32 devices in a mesh: ctx: 8 (over y, x, core), head: 4 (over z).
Axes of the slice: x: 2, y: 2, z: 4, core: 2. Of those that a mesh axis runs over, the one named last changes fastest.
Arguments:
- query_vectors: bfloat16 [1024, 4096], P('ctx', 'head'), may hold values from -6 to 6
- key_vectors: bfloat16 [1024, 4096], P('ctx', 'head'), may hold values from -1.5 to 1.5
- value_vectors: bfloat16 [1024, 4096], P('ctx', 'head'), may hold values from -6 to 6
- log_decay: float32 [32, 1024], P('head', 'ctx'), may hold values from -2 to 0, as said below
- residual: bfloat16 [1024, 3072], P('ctx'), may hold values from -6 to 6
- out_weight: bfloat16 [4096, 3072], P('head', 'ctx'), may hold values from -0.09375 to 0.09375
- attn_gain: float32 [4096], P('head'), may hold values from 0.1 to 1.9
- moe_gain: float32 [3072], replicated, may hold values from 0.1 to 1.9
- router: float32 [3072, 8], replicated, may hold values from -0.109375 to 0.109375
- w_gate: bfloat16 [8, 3072, 4608], P('ctx', None, 'head'), may hold values from -0.109375 to 0.109375
- w_up: bfloat16 [8, 3072, 4608], P('ctx', None, 'head'), may hold values from -0.109375 to 0.109375
- w_down: bfloat16 [8, 4608, 3072], P('ctx', 'head'), may hold values from -0.09375 to 0.09375
- expert_ids: int32 [1024, 2], P('ctx'), may hold values from 0 to 7, all different within a row; in each aligned block of 128 rows (0 to 127, 128 to 255, ...) at most 64 rows name the same one
Outputs:
- final_out: bfloat16 [1024, 3072], P('ctx', 'head')
The draws below stay inside these ranges and needn't reach their ends.
Inputs may be any that keep to these rules, and one draw needn't show every extreme that they name: `expert_ids`: each row names 2 different experts. In each aligned block of 128 rows no expert is named by more than 64 rows, and in every draw some expert is named by exactly 64 rows of some block. `log_decay`: every entry is negative.
All inputs are finite; a program needn't handle non-finite values.
Results may differ from the reference program's by a relative error of at most 0.022.
Values may be sent and summed in bfloat16 or wider, within the bound.
A program may use at most 128 MiB of HBM per device.

```python
import math
from functools import partial
import jax
import jax.numpy as jnp
import numpy as np
from jax import lax

D = 3072
HEAD_COUNT = 32
HDIM = 128
FF = 4608
TOP = 2
TOK_DEV = 128
EXPERTS = 8
CAP = 64
SEQUENCE_LENGTH = 1024
N_HEAD = 4


def draw_log_decay(key, part):
    random_keys = jax.random.split(key, 7)
    fast_share = 0.5
    fast_heads = jax.random.uniform(random_keys[0], (HEAD_COUNT, 1)) < fast_share
    fast_rate = jnp.exp(jax.random.uniform(random_keys[1], (HEAD_COUNT, 1), minval=math.log(1.0 / 50.0), maxval=math.log(1.0 / 30.0)))
    slow_rate = jnp.exp(jax.random.uniform(random_keys[2], (HEAD_COUNT, 1), minval=math.log(0.2), maxval=math.log(0.8))) / SEQUENCE_LENGTH
    baseline_decay = jnp.where(fast_heads, fast_rate, slow_rate)
    blocks_total = SEQUENCE_LENGTH // TOK_DEV
    block_factor = jnp.exp(jax.random.uniform(random_keys[3], (HEAD_COUNT, blocks_total, 1), minval=math.log(0.5), maxval=math.log(2.0)))
    block_factor = jnp.broadcast_to(block_factor, (HEAD_COUNT, blocks_total, TOK_DEV)).reshape(HEAD_COUNT, SEQUENCE_LENGTH)
    jitter_amount = jax.random.uniform(random_keys[4], (HEAD_COUNT, SEQUENCE_LENGTH), minval=0.5, maxval=1.5)
    spike_positions = jax.random.randint(random_keys[5], (HEAD_COUNT, 2), 0, SEQUENCE_LENGTH)
    spike_magnitude = jax.random.uniform(random_keys[6], (HEAD_COUNT, 2), minval=math.log(0.5), maxval=math.log(0.8))
    position_index = jax.lax.broadcasted_iota(jnp.int32, (HEAD_COUNT, SEQUENCE_LENGTH, 2), 1)
    spike_events = jnp.sum(jnp.where(position_index == spike_positions[:, None, :], spike_magnitude[:, None, :], 0.0), axis=2)
    return (-(baseline_decay * block_factor * jitter_amount) + spike_events).astype(jnp.float32)


def levels(own_key, extent, pieces, low, top_value):
    def one(dim, blocks):
        heights = jax.random.uniform(jax.random.fold_in(jax.random.fold_in(own_key, 6), dim), (blocks,), jnp.float32, low / len(pieces), top_value / len(pieces))
        return jnp.repeat(jnp.exp(heights), extent[dim] // blocks).reshape((-1,) + (1,) * (len(extent) - dim - 1))

    gain = one(*pieces[0])
    for cut in pieces[1:]:
        gain = gain * one(*cut)
    return gain


def routed_block(stream_key, own, number, rows, number_of, top, reach, skew):
    ranking = jax.random.permutation(stream_key, number_of)
    heavy_load, common = portions_of(number_of, rows * top, reach, skew, True), portions_of(number_of, rows * top, reach, skew, False)
    places = jnp.arange(number_of)

    def named(sizes, offset_by):
        used = int((sizes > 0).sum())
        fixed = max(1, used // 4)
        moved = fixed + (places - fixed + offset_by * (used - fixed)) % max(1, number_of - fixed)
        return jnp.zeros((number_of,), jnp.int32).at[ranking[jnp.where(places < fixed, places, moved)]].set(jnp.asarray(sizes, jnp.int32))

    sizes = jnp.where(number % 4 == 0, named(heavy_load, number // 4), named(common, number - number // 4 - 1))
    mixed = jax.random.permutation(jax.random.fold_in(own, 3), number_of)
    giver, sink = mixed[0:number_of // 2 * 2:2], mixed[1:number_of // 2 * 2:2]
    margin = jnp.minimum(sizes[giver] - 1, reach - sizes[sink]) // 2
    margin = jnp.where((giver == ranking[0]) | (sink == ranking[0]) | (sizes[sink] == 0), 0, jnp.maximum(margin, 0))
    moved = jax.random.randint(jax.random.fold_in(own, 4), (number_of // 2,), 0, 1 << 20) % (margin + 1)
    sizes = sizes.at[giver].add(-moved).at[sink].add(moved)
    labels = jnp.searchsorted(jnp.cumsum(sizes), jnp.arange(rows * top), side="right").astype(jnp.int32)
    table = labels.reshape(top, rows).T
    table = table[jax.random.permutation(jax.random.fold_in(own, 1), rows)]
    offset_by = jax.random.randint(jax.random.fold_in(own, 2), (rows, 1), 0, top)
    return jnp.take_along_axis(table, (jnp.arange(top)[None, :] + offset_by) % top, axis=1)


def portions_of(amount, total, bound, slope, full):
    portions = [(1 << 20) // math.isqrt(rank ** slope) + 1 for rank in range(1, amount + 1)]
    largest = bound if full else min(bound, max(-(-total // amount), total * portions[0] // sum(portions)))
    least = 1 if total - largest >= amount - 1 else 0
    given, rest = [largest] + [least] * (amount - 1), total - largest - least * (amount - 1)
    while rest > 0:
        candidates = [i for i in range(1, amount) if given[i] < largest] or [i for i in range(1, amount) if given[i] < bound]
        pool, budget = sum([portions[i] for i in candidates]), rest
        for i in candidates:
            more = min(bound - given[i], max(1, budget * portions[i] // pool), rest)
            given[i] = given[i] + more
            rest = rest - more
    return np.array(given)


def bell_draw(stream_key, dims, deviation, reach, cuts=(), held_as=jnp.bfloat16):
    loudness = levels(stream_key, dims, cuts, -0.22, 0.18) if cuts else 1.0
    drawn = jax.random.normal(stream_key, dims, jnp.float32) * deviation * loudness
    return jnp.minimum(jnp.maximum(drawn, -reach), reach).astype(held_as)


def setup_inputs(seed: int = 0) -> dict:
    arg_keys = jax.random.split(jax.random.key(seed), 14)
    query_vectors = bell_draw(arg_keys[0], (SEQUENCE_LENGTH, HEAD_COUNT * HDIM), 1.0, 6.0, ((0, 8), (1, 4)))
    key_vectors = bell_draw(arg_keys[1], (SEQUENCE_LENGTH, HEAD_COUNT * HDIM), 0.25, 1.5, ((0, 8), (1, 4)))
    value_vectors = bell_draw(arg_keys[2], (SEQUENCE_LENGTH, HEAD_COUNT * HDIM), 1.0, 6.0, ((0, 8), (1, 4)))
    log_decay = draw_log_decay(jax.random.fold_in(arg_keys[13], 71), 0)
    residual = bell_draw(arg_keys[4], (SEQUENCE_LENGTH, D), 1.0, 6.0, ((0, 8),))
    out_weight = bell_draw(arg_keys[5], (HEAD_COUNT * HDIM, D), (HEAD_COUNT * HDIM) ** -0.5, 0.09375, ((0, 4), (1, 8)))
    attn_gain = jnp.clip(1.0 + 0.18 * jax.random.normal(arg_keys[6], (HEAD_COUNT * HDIM,), jnp.float32), 0.1, 1.9)
    moe_gain = jnp.clip(1.0 + 0.18 * jax.random.normal(arg_keys[7], (D,), jnp.float32), 0.1, 1.9)
    router = bell_draw(arg_keys[8], (D, EXPERTS), D ** -0.5, 0.109375, (), jnp.float32)
    w_gate = bell_draw(arg_keys[9], (EXPERTS, D, FF), D ** -0.5, 0.109375, ((0, 8), (2, 4)))
    w_up = bell_draw(arg_keys[10], (EXPERTS, D, FF), D ** -0.5, 0.109375, ((0, 8), (2, 4)))
    w_down = bell_draw(arg_keys[11], (EXPERTS, FF, D), FF ** -0.5, 0.09375, ((0, 8), (1, 4)))
    expert_ids_keys = jax.random.split(jax.random.fold_in(arg_keys[12], 1), SEQUENCE_LENGTH // TOK_DEV)
    expert_ids_turns = jax.random.permutation(jax.random.fold_in(arg_keys[12], 3), SEQUENCE_LENGTH // TOK_DEV)
    expert_ids = jax.vmap(lambda own, number: routed_block(jax.random.fold_in(arg_keys[12], 2), own, number, TOK_DEV, EXPERTS, TOP, CAP, 2))(expert_ids_keys, expert_ids_turns).reshape((SEQUENCE_LENGTH, TOP))
    return dict(query_vectors=query_vectors, key_vectors=key_vectors, value_vectors=value_vectors, log_decay=log_decay, residual=residual, out_weight=out_weight, attn_gain=attn_gain, moe_gain=moe_gain, router=router, w_gate=w_gate, w_up=w_up, w_down=w_down, expert_ids=expert_ids)


PRECISE = lax.Precision.HIGHEST

def block_attention(query_block, key_block, value_block, decay_block, state_before):
    running = jnp.cumsum(decay_block, axis=1)
    length_here = decay_block.shape[1]
    row_index = lax.broadcasted_iota(jnp.int32, (length_here, length_here), 0)
    col_index = lax.broadcasted_iota(jnp.int32, (length_here, length_here), 1)
    causal = (col_index <= row_index)[None]
    spread = jnp.where(causal, running[:, :, None] - running[:, None, :], 0.0)
    decay_weights = jnp.where(causal, jnp.exp(spread), 0.0)
    scores = jnp.einsum('htd,hsd->hts', query_block, key_block, precision=PRECISE) * decay_weights
    inside_part = jnp.einsum('hts,hse->hte', scores, value_block, precision=PRECISE)
    outside_part = jnp.exp(running)[:, :, None] * jnp.einsum('htd,hde->hte', query_block, state_before, precision=PRECISE)
    final_log = running[:, -1]
    tail_decay = jnp.exp(final_log[:, None] - running)
    local_state = jnp.einsum('hsd,hse->hde', key_block * tail_decay[:, :, None], value_block, precision=PRECISE)
    state_after = jnp.exp(final_log)[:, None, None] * state_before + local_state
    return (inside_part + outside_part, state_after)

def route_tokens(logits, expert_ids, experts_total):
    onehot = expert_ids[:, :, None] == lax.broadcasted_iota(jnp.int32, (1, 1, experts_total), 2)
    chosen = lax.optimization_barrier(jnp.sum(jnp.where(onehot, logits[:, None, :], 0.0), axis=2))
    leading = jax.nn.sigmoid(chosen[:, 0] - chosen[:, 1])
    gate_weights = jnp.stack([leading, 1.0 - leading], axis=1)
    marked = onehot.reshape(-1, experts_total).astype(jnp.int32)
    earlier = jnp.cumsum(marked, axis=0) - marked
    slot_index = lax.optimization_barrier(jnp.sum(earlier * marked, axis=1)).reshape(expert_ids.shape).astype(jnp.int32)
    return (gate_weights, slot_index)

def reference(query_vectors, key_vectors, value_vectors, log_decay, residual, out_weight, attn_gain, moe_gain, router, w_gate, w_up, w_down, expert_ids):
    blocks_total = SEQUENCE_LENGTH // TOK_DEV

    def split_heads(matrix_in):
        return matrix_in.astype(jnp.float32).reshape(blocks_total, TOK_DEV, HEAD_COUNT, HDIM).transpose(0, 2, 1, 3)
    decays = log_decay.reshape(HEAD_COUNT, blocks_total, TOK_DEV).transpose(1, 0, 2)

    def advance(state_now, inputs):
        attended, state_next = block_attention(inputs[0], inputs[1], inputs[2], inputs[3], state_now)
        return (state_next, attended)
    initial = jnp.zeros((HEAD_COUNT, HDIM, HDIM), jnp.float32)
    _, attended = lax.scan(advance, initial, (split_heads(query_vectors), split_heads(key_vectors), split_heads(value_vectors), decays))
    attended = attended.transpose(0, 2, 1, 3).reshape(SEQUENCE_LENGTH, HEAD_COUNT, HDIM)
    square_mean = lax.optimization_barrier(jnp.mean(attended * attended, axis=2, keepdims=True))
    heads_normed = (attended * lax.rsqrt(square_mean + 1e-05) * attn_gain.reshape(1, HEAD_COUNT, HDIM)).astype(jnp.bfloat16)
    heads_normed = heads_normed.reshape(SEQUENCE_LENGTH, HEAD_COUNT * HDIM)
    projected = jnp.dot(heads_normed, out_weight, preferred_element_type=jnp.float32)
    mixed_rows = (residual.astype(jnp.float32) + projected).astype(jnp.bfloat16)
    mixed_wide = mixed_rows.astype(jnp.float32)
    inv_rms = lax.rsqrt(lax.optimization_barrier(jnp.mean(mixed_wide * mixed_wide, axis=1, keepdims=True)) + 1e-06)
    scaled = mixed_wide * moe_gain[None, :]
    moe_in = (scaled * inv_rms).astype(jnp.bfloat16)
    logits = inv_rms * jnp.dot(scaled, router, precision=PRECISE)
    ids_blocks = expert_ids.reshape(blocks_total, TOK_DEV, TOP).astype(jnp.int32)
    gate_weights, slot_index = jax.vmap(partial(route_tokens, experts_total=EXPERTS))(logits.reshape(blocks_total, TOK_DEV, EXPERTS), ids_blocks)
    block_number = lax.broadcasted_iota(jnp.int32, (blocks_total, TOK_DEV, TOP), 0)
    token_number = block_number * TOK_DEV + lax.broadcasted_iota(jnp.int32, (blocks_total, TOK_DEV, TOP), 1)
    row_table = jnp.full((EXPERTS, blocks_total, CAP), SEQUENCE_LENGTH, jnp.int32)
    row_table = row_table.at[ids_blocks, block_number, slot_index].set(token_number)
    padded_in = jnp.concatenate([moe_in, jnp.zeros((1, D), jnp.bfloat16)], axis=0)
    group_width = FF // N_HEAD

    def run_expert(inputs):
        index_rows, gate_matrix, up_matrix, down_matrix = inputs
        gathered = padded_in[index_rows.reshape(-1)]
        hidden = (jax.nn.silu(jnp.dot(gathered, gate_matrix, preferred_element_type=jnp.float32)) * jnp.dot(gathered, up_matrix, preferred_element_type=jnp.float32)).astype(jnp.bfloat16)
        summed = jnp.zeros((gathered.shape[0], D), jnp.float32)
        for group_index in range(N_HEAD):
            lower_edge = group_index * group_width
            partial_sum = jnp.dot(hidden[:, lower_edge:lower_edge + group_width], down_matrix[lower_edge:lower_edge + group_width], preferred_element_type=jnp.float32)
            partial_sum = lax.optimization_barrier(partial_sum.astype(jnp.bfloat16))
            summed = summed + partial_sum.astype(jnp.float32)
        return summed.astype(jnp.bfloat16)
    expert_out = lax.map(run_expert, (row_table, w_gate, w_up, w_down))
    flat_out = expert_out.reshape(EXPERTS * blocks_total * CAP, D)
    pick_index = (ids_blocks * (blocks_total * CAP) + block_number * CAP + slot_index).reshape(SEQUENCE_LENGTH, TOP).astype(jnp.int32)
    picked = flat_out[pick_index].astype(jnp.float32)
    gate_flat = gate_weights.reshape(SEQUENCE_LENGTH, TOP)
    final_out = mixed_wide + gate_flat[:, 0:1] * picked[:, 0] + gate_flat[:, 1:2] * picked[:, 1]
    return final_out.astype(jnp.bfloat16)
```

```python
import functools

import jax
import jax.numpy as jnp
from jax import lax
from jax.experimental import pallas as pl
from jax.experimental.pallas import tpu as pltpu
from jax.sharding import PartitionSpec as P

TOP = 2


PRECISE = lax.Precision.HIGHEST


def entering(value, axis, combine, identity):
    peers, index = (lax.axis_size(axis), lax.axis_index(axis))
    everything = jax.tree.map(
        lambda part, kind: lax.all_gather(part.astype(kind), axis),
        value,
        (jnp.bfloat16, jnp.bfloat16),
    )
    start = jax.tree.map(
        lambda part, zero: jnp.broadcast_to(jnp.asarray(zero, part.dtype), part.shape),
        value,
        identity,
    )

    def step(k, before):
        reached = k < index
        new = combine(
            before, jax.tree.map(lambda part, own: part[k].astype(own.dtype), everything, value)
        )
        return jax.tree.map(lambda a, b: jnp.where(reached, a, b), new, before)

    return lax.fori_loop(0, peers, step, start)


def local_attention(query_block, key_block, value_block, decay_block):
    running = jnp.cumsum(decay_block, axis=1)
    length_here = decay_block.shape[1]
    row_index = lax.broadcasted_iota(jnp.int32, (length_here, length_here), 0)
    col_index = lax.broadcasted_iota(jnp.int32, (length_here, length_here), 1)
    causal = (col_index <= row_index)[None]
    spread = jnp.where(causal, running[:, :, None] - running[:, None, :], 0.0)
    decay_weights = jnp.where(causal, jnp.exp(spread), 0.0)
    scores = jnp.einsum("htd,hsd->hts", query_block, key_block, precision=PRECISE) * decay_weights
    inside_part = jnp.einsum("hts,hse->hte", scores, value_block, precision=PRECISE)
    final_log = running[:, -1]
    tail_decay = jnp.exp(final_log[:, None] - running)
    local_state = jnp.einsum(
        "hsd,hse->hde", key_block * tail_decay[:, :, None], value_block, precision=PRECISE
    )
    return (inside_part, running, local_state, final_log)


def route_tokens(logits, expert_ids, experts_total):
    onehot = expert_ids[:, :, None] == lax.broadcasted_iota(jnp.int32, (1, 1, experts_total), 2)
    chosen = jnp.sum(jnp.where(onehot, logits[:, None, :], 0.0), axis=2)
    leading = jax.nn.sigmoid(chosen[:, 0] - chosen[:, 1])
    gate_weights = jnp.stack([leading, 1.0 - leading], axis=1)
    marked = onehot.reshape(-1, experts_total).astype(jnp.int32)
    earlier = jnp.cumsum(marked, axis=0) - marked
    slot_index = jnp.sum(earlier * marked, axis=1).reshape(expert_ids.shape)
    return (gate_weights, slot_index)


def link_states(earlier, later):
    return (earlier[0] + later[0], jnp.exp(later[0])[:, None, None] * earlier[1] + later[1])


def general_body(
    query_vectors,
    key_vectors,
    value_vectors,
    log_decay,
    residual,
    out_weight,
    attn_gain,
    moe_gain,
    router,
    w_gate,
    w_up,
    w_down,
    expert_ids,
):
    token_count = query_vectors.shape[0]
    heads_here = log_decay.shape[0]
    head_size = query_vectors.shape[1] // heads_here

    def split_heads(matrix_in):
        return (
            matrix_in.astype(jnp.float32)
            .reshape(token_count, heads_here, head_size)
            .transpose(1, 0, 2)
        )

    query_heads = split_heads(query_vectors)
    inside_part, running, local_state, final_log = local_attention(
        query_heads, split_heads(key_vectors), split_heads(value_vectors), log_decay
    )
    identity = (jnp.zeros_like(final_log), jnp.zeros_like(local_state))
    _, prior_state = entering((final_log, local_state), "ctx", link_states, identity)
    outside_part = jnp.exp(running)[:, :, None] * jnp.einsum(
        "htd,hde->hte", query_heads, prior_state, precision=PRECISE
    )
    attended = inside_part + outside_part
    square_mean = jnp.mean(attended * attended, axis=2, keepdims=True)
    heads_normed = (
        attended * lax.rsqrt(square_mean + 1e-05) * attn_gain.reshape(heads_here, 1, head_size)
    )
    heads_normed = (
        heads_normed.astype(jnp.bfloat16)
        .transpose(1, 0, 2)
        .reshape(token_count, heads_here * head_size)
    )
    partial_out = jnp.dot(
        heads_normed,
        lax.all_gather(out_weight, "ctx", axis=1, tiled=True),
        preferred_element_type=jnp.float32,
    )
    model_width = residual.shape[1]
    experts_total = router.shape[1]
    capacity = 2 * token_count * TOP // experts_total
    slice_width = model_width // lax.axis_size("head")
    slice_start = lax.axis_index("head") * slice_width
    projected = lax.psum(partial_out.astype(jnp.bfloat16), "head").astype(jnp.float32)
    mixed_rows = (residual.astype(jnp.float32) + projected).astype(jnp.bfloat16)
    mixed_wide = mixed_rows.astype(jnp.float32)
    inv_rms = lax.rsqrt(jnp.mean(mixed_wide * mixed_wide, axis=1, keepdims=True) + 1e-06)
    scaled = mixed_wide * moe_gain[None, :]
    moe_in = (scaled * inv_rms).astype(jnp.bfloat16)
    logits = inv_rms * jnp.dot(scaled, router, precision=PRECISE)
    base_slice = lax.dynamic_slice_in_dim(mixed_wide, slice_start, slice_width, 1)
    gate_weights, slot_index = route_tokens(logits, expert_ids, experts_total)
    target = (expert_ids * capacity + slot_index).reshape(-1)
    width_here = moe_in.shape[1]
    source = jnp.repeat(moe_in, TOP, axis=0)
    packed = jnp.zeros((experts_total * capacity, width_here), jnp.bfloat16).at[target].set(source)
    arrived = lax.all_to_all(
        packed.reshape(experts_total, capacity, width_here),
        "ctx",
        split_axis=0,
        concat_axis=0,
        tiled=True,
    )
    flat_rows = arrived.reshape(-1, model_width)
    gate_part = jnp.dot(flat_rows, w_gate[0], preferred_element_type=jnp.float32)
    up_part = jnp.dot(flat_rows, w_up[0], preferred_element_type=jnp.float32)
    hidden = (jax.nn.silu(gate_part) * up_part).astype(jnp.bfloat16)
    partial_down = jnp.dot(hidden, w_down[0], preferred_element_type=jnp.float32).reshape(
        arrived.shape
    )
    returned = lax.all_to_all(
        lax.all_to_all(
            partial_down.astype(jnp.bfloat16)[None], "ctx", split_axis=1, concat_axis=1, tiled=True
        ),
        "head",
        split_axis=3,
        concat_axis=0,
        tiled=True,
    )
    expert_out = jnp.sum(returned.astype(jnp.float32), axis=0).astype(jnp.bfloat16)
    lookup = expert_out.reshape(experts_total * capacity, slice_width)
    picked = lookup[target].reshape(token_count, TOP, slice_width).astype(jnp.float32)
    final_out = (
        base_slice + gate_weights[:, 0:1] * picked[:, 0] + gate_weights[:, 1:2] * picked[:, 1]
    )
    return final_out.astype(jnp.bfloat16)


MESH = pl.DeviceIdType.MESH
ANY = pl.BlockSpec(memory_space=pl.ANY)
VMEM = pl.BlockSpec(memory_space=pltpu.VMEM)


def plane_peers():
    me = lax.axis_index("ctx")
    core, x, y = me % 2, (me // 2) % 2, me // 4

    def at(c, a, b):
        return (b * 2 + a) * 2 + c

    return (
        me,
        at(1 - core, x, y),
        at(core, 1 - x, y),
        at(core, x, 1 - y),
        at(core, 1 - x, 1 - y),
    )


def greet(axes_and_peers):
    barrier = pltpu.get_barrier_semaphore()
    for axis, peer in axes_and_peers:
        pl.semaphore_signal(barrier, inc=1, device_id={axis: peer}, device_id_type=MESH)
    pl.semaphore_wait(barrier, len(axes_and_peers))


def gather_kernel(count, *refs):
    blocks, outs = refs[:count], refs[count : 2 * count]
    send, recv, local = refs[2 * count :]
    me, sib, xn, yn, dg = plane_peers()
    greet([("ctx", sib), ("ctx", xn), ("ctx", yn)])

    def copy(i, step, src, dst, peer):
        return pltpu.make_async_remote_copy(
            src_ref=src,
            dst_ref=dst,
            send_sem=send.at[i, step],
            recv_sem=recv.at[i, step],
            device_id={"ctx": peer},
            device_id_type=MESH,
        )

    plans, own = [], []
    for i, (block, out) in enumerate(zip(blocks, outs)):
        half = block.shape[0] // 2
        top, low = pl.ds(0, half), pl.ds(half, half)
        plan = [
            copy(i, 0, block, out.at[me], sib),
            copy(i, 1, block, out.at[me], xn),
            copy(i, 2, block, out.at[me], yn),
            copy(i, 3, out.at[xn, top], out.at[xn, top], yn),
            copy(i, 4, out.at[xn], out.at[xn], sib),
            copy(i, 5, out.at[yn, low], out.at[yn, low], xn),
            copy(i, 6, out.at[yn], out.at[yn], sib),
            copy(i, 7, out.at[dg, top], out.at[dg, top], sib),
            copy(i, 8, out.at[dg, low], out.at[dg, low], sib),
        ]
        plans.append(plan)
        for step in (1, 2, 0):
            plan[step].start()
        mine = pltpu.make_async_copy(block, out.at[me], local.at[i])
        mine.start()
        own.append(mine)
    for got, onward in ((1, (3, 4)), (2, (5, 6)), (3, (7,)), (5, (8,))):
        for plan in plans:
            plan[got].wait_recv()
            for step in onward:
                plan[step].start()
    for plan, mine in zip(plans, own):
        for step in (0, 4, 6, 7, 8):
            plan[step].wait_recv()
        for step in range(9):
            plan[step].wait_send()
        mine.wait()


def plane_gather(collective_id, *blocks):
    count = len(blocks)
    ctx = lax.axis_size("ctx")
    return pl.pallas_call(
        functools.partial(gather_kernel, count),
        out_shape=[jax.ShapeDtypeStruct((ctx,) + b.shape, b.dtype) for b in blocks],
        in_specs=[ANY] * count,
        out_specs=[ANY] * count,
        scratch_shapes=[
            pltpu.SemaphoreType.DMA((count, 9)),
            pltpu.SemaphoreType.DMA((count, 9)),
            pltpu.SemaphoreType.DMA((count,)),
        ],
        compiler_params=pltpu.CompilerParams(collective_id=collective_id, has_side_effects=True),
        name="plane_gather",
    )(*blocks)


def block_order(me, sib, xn, yn, dg):
    def other_core(index):
        return index + 1 - 2 * (index % 2)

    return (me, sib, xn, yn, other_core(xn), other_core(yn), dg, other_core(dg))


def z_order():
    z = lax.axis_index("head")
    return (z + 1 - 2 * (z % 2), z + 2 - 4 * (z // 2), 3 - z)


def sender(send, recv):
    def copy(at, src, dst, axis, peer):
        return pltpu.make_async_remote_copy(
            src_ref=src,
            dst_ref=dst,
            send_sem=send.at[at],
            recv_sem=recv.at[at],
            device_id={axis: peer},
            device_id_type=MESH,
        )

    return copy


GATHER, TO_Z, TO_COLS, ROWS_Z, BASE_Z, SPREAD = 0, 9, 33, 41, 44, 47


def spread_kernel(
    normed, weight, residual, gain, router, ids, base, out,
    rows, part, from_z, summed, by_cols, mixed, piece, send, recv, local,
):
    me, sib, xn, yn, dg = plane_peers()
    z = lax.axis_index("head")
    blocks, zs = block_order(me, sib, xn, yn, dg), z_order()
    greet([("ctx", b) for b in blocks[1:]] + [("head", p) for p in zs])
    copy = sender(send, recv)
    f32, bf16 = jnp.float32, jnp.bfloat16
    share, model_width = residual.shape
    width = weight.shape[1]
    half = normed.shape[0] // 2
    top, low = pl.ds(0, half), pl.ds(half, half)

    plan = [
        copy(0, normed, rows.at[me], "ctx", sib),
        copy(1, normed, rows.at[me], "ctx", xn),
        copy(2, normed, rows.at[me], "ctx", yn),
        copy(3, rows.at[xn, top], rows.at[xn, top], "ctx", yn),
        copy(4, rows.at[xn], rows.at[xn], "ctx", sib),
        copy(5, rows.at[yn, low], rows.at[yn, low], "ctx", xn),
        copy(6, rows.at[yn], rows.at[yn], "ctx", sib),
        copy(7, rows.at[dg, top], rows.at[dg, top], "ctx", sib),
        copy(8, rows.at[dg, low], rows.at[dg, low], "ctx", sib),
    ]
    for step in (1, 2, 0):
        plan[step].start()
    sent = list(plan)
    z_in = []

    def project(i, block):
        product = jnp.dot(block, weight[...], preferred_element_type=f32).astype(bf16)
        for k in range(len(zs) + 1):
            part[i, k] = product[k * share : (k + 1) * share]
        z_in.append([])
        for d, peer in enumerate(zs):
            out_copy = copy(
                TO_Z + 3 * i + d, part.at[i, peer], from_z.at[i, d], "head", peer
            )
            out_copy.start()
            z_in[i].append(out_copy)
            sent.append(out_copy)

    def arrived(*steps):
        for step in steps:
            plan[step].wait_recv()

    project(0, normed[...])
    arrived(0)
    project(1, rows[sib])
    arrived(1)
    plan[3].start()
    plan[4].start()
    project(2, rows[xn])
    arrived(2)
    plan[5].start()
    plan[6].start()
    project(3, rows[yn])
    arrived(4)
    project(4, rows[blocks[4]])
    arrived(6)
    project(5, rows[blocks[5]])
    arrived(3)
    plan[7].start()
    arrived(5)
    plan[8].start()
    project(6, rows[dg])
    arrived(7, 8)
    project(7, rows[blocks[7]])

    col_copies = []
    for i, block in enumerate(blocks):
        total = part[i, z].astype(f32)
        for d in range(3):
            z_in[i][d].wait_recv()
            total += from_z[i, d].astype(f32)
        summed[i] = total.astype(bf16)
        if i:
            col_copies.append(
                copy(TO_COLS + i, summed.at[i], by_cols.at[me], "ctx", block)
            )
            col_copies[-1].start()
    by_cols[me] = summed[0]
    for each in col_copies:
        each.wait_recv()
    sent += col_copies

    per = model_width // (len(zs) + 1) // width
    squares = jnp.zeros((share, 1), f32)
    for k in range(model_width // width):
        cols = slice(k * width, (k + 1) * width)
        whole = (residual[:, cols].astype(f32) + by_cols[k].astype(f32)).astype(bf16)
        mixed[k // per, :, (k % per) * width : (k % per + 1) * width] = whole
        wide = whole.astype(f32)
        squares += jnp.sum(wide * wide, axis=1, keepdims=True)
    inv_rms = lax.rsqrt(squares / model_width + 1e-06)
    experts_total = router.shape[0]
    logits = [jnp.zeros((share, 1), f32)] * experts_total
    slice_width = per * width
    for k in range(len(zs) + 1):
        cols = slice(k * slice_width, (k + 1) * slice_width)
        scaled = mixed[k].astype(f32) * gain[:, cols]
        piece[:, cols] = (scaled * inv_rms).astype(bf16)
        for e in range(experts_total):
            logits[e] += jnp.sum(scaled * router[e : e + 1, cols], axis=1, keepdims=True)
    first, second = ids[:, 0:1], ids[:, 1:2]
    ahead = jnp.zeros((share, 1), f32)
    for e in range(experts_total):
        ahead += jnp.where(first == e, logits[e], 0.0) - jnp.where(second == e, logits[e], 0.0)
    leading = jax.nn.sigmoid(ahead * inv_rms)
    big = leading.astype(bf16).astype(f32)
    middle = (leading - big).astype(bf16).astype(f32)
    small = leading - big - middle
    lane = lax.broadcasted_iota(jnp.int32, (share, 128), 1)
    notes = jnp.zeros((share, 128), f32)
    for k, value in enumerate((first.astype(f32), second.astype(f32), big, middle, small)):
        notes = jnp.where(lane == k, value, notes)
    piece[:, model_width:] = notes.astype(bf16)

    z_copies, base_copies = [], []
    quarter = share // 2
    upper, lower = pl.ds(0, quarter), pl.ds(quarter, quarter)

    def spread(j, source, k):
        s = SPREAD + 9 * j
        steps = [
            copy(s, source, out.at[me, k], "ctx", sib),
            copy(s + 1, source, out.at[me, k], "ctx", xn),
            copy(s + 2, source, out.at[me, k], "ctx", yn),
            copy(s + 3, out.at[xn, k, upper], out.at[xn, k, upper], "ctx", yn),
            copy(s + 4, out.at[xn, k], out.at[xn, k], "ctx", sib),
            copy(s + 5, out.at[yn, k, lower], out.at[yn, k, lower], "ctx", xn),
            copy(s + 6, out.at[yn, k], out.at[yn, k], "ctx", sib),
            copy(s + 7, out.at[dg, k, upper], out.at[dg, k, upper], "ctx", sib),
            copy(s + 8, out.at[dg, k, lower], out.at[dg, k, lower], "ctx", sib),
        ]
        for step in (1, 2, 0):
            steps[step].start()
        return steps

    def relay(steps):
        for got, onward in ((1, (3, 4)), (2, (5, 6)), (3, (7,)), (5, (8,))):
            steps[got].wait_recv()
            for step in onward:
                steps[step].start()

    for d, peer in enumerate(zs):
        z_copies.append(copy(ROWS_Z + d, piece, out.at[me, z], "head", peer))
        z_copies[-1].start()
    runs = [spread(0, piece, z)]
    mine = pltpu.make_async_copy(piece, out.at[me, z], local.at[0])
    mine.start()
    own_base = pltpu.make_async_copy(mixed.at[z], base.at[z], local.at[1])
    own_base.start()
    for d, peer in enumerate(zs):
        z_copies[d].wait_recv()
        runs.append(spread(d + 1, out.at[me, peer], peer))
        relay(runs[d])
    for d, peer in enumerate(zs):
        base_copies.append(copy(BASE_Z + d, mixed.at[peer], base.at[z], "head", peer))
        base_copies[-1].start()
    relay(runs[3])
    for steps in runs:
        for step in (0, 4, 6, 7, 8):
            steps[step].wait_recv()
        sent += steps
    for each in base_copies:
        each.wait_recv()
    for each in sent + z_copies + base_copies:
        each.wait_send()
    mine.wait()
    own_base.wait()


def spread_rows(normed, weight, residual_rows, gain, router, ids):
    ctx, planes = lax.axis_size("ctx"), lax.axis_size("head")
    tokens, depth = normed.shape
    width = weight.shape[1]
    share, model_width = residual_rows.shape
    dma, bf16 = pltpu.SemaphoreType.DMA, jnp.bfloat16
    return pl.pallas_call(
        spread_kernel,
        out_shape=[
            jax.ShapeDtypeStruct((planes, share, model_width // planes), bf16),
            jax.ShapeDtypeStruct((ctx, planes, share, model_width + 128), bf16),
        ],
        in_specs=[VMEM] * 6,
        out_specs=[ANY, ANY],
        scratch_shapes=[
            pltpu.VMEM((ctx, tokens, depth), bf16),
            pltpu.VMEM((ctx, planes, share, width), bf16),
            pltpu.VMEM((ctx, planes - 1, share, width), bf16),
            pltpu.VMEM((ctx, share, width), bf16),
            pltpu.VMEM((ctx, share, width), bf16),
            pltpu.VMEM((planes, share, model_width // planes), bf16),
            pltpu.VMEM((share, model_width + 128), bf16),
            dma((SPREAD + 9 * planes,)),
            dma((SPREAD + 9 * planes,)),
            dma((2,)),
        ],
        compiler_params=pltpu.CompilerParams(
            collective_id=2, has_side_effects=True, vmem_limit_bytes=40 << 20
        ),
        name="spread_rows",
    )(normed, weight, residual_rows, gain, router, ids)


PAIR, SUMS, SLICES = 0, 4, 28
TILE = 256


def expert_kernel(
    tokens, w_gate, w_up, w_down, base, out,
    toks, wide, down, picked, slot_gate, hidden, theirs, ours, pair, onehots,
    ahead, across, landed, total, from_z, send, recv, load,
):
    me, sib, xn, yn, dg = plane_peers()
    z = lax.axis_index("head")
    zs = z_order()
    chunks = zs + (z,)
    f32, bf16 = jnp.float32, jnp.bfloat16
    count, model_width = picked.shape[0] // 8, picked.shape[1]
    units = hidden.shape[1]
    tiles = units // TILE

    def other_core(index):
        return index + 1 - 2 * (index % 2)

    away = (other_core(dg), other_core(xn), other_core(yn), sib)
    here = (dg, xn, yn, me)
    order = away + here
    token_loads = [
        pltpu.make_async_copy(tokens.at[b], toks.at[i], load.at[i]) for i, b in enumerate(order)
    ]
    for each in token_loads:
        each.start()
    weight_loads = []
    for j in range(tiles):
        for k, matrix in enumerate((w_gate, w_up)):
            weight_loads.append(
                pltpu.make_async_copy(
                    matrix.at[:, pl.ds(j * TILE, TILE)],
                    wide.at[2 * j + k],
                    load.at[8 + 2 * j + k],
                )
            )
    rest = units - tiles * TILE
    for k, matrix in enumerate((w_gate, w_up)):
        weight_loads.append(
            pltpu.make_async_copy(
                matrix.at[:, pl.ds(tiles * TILE, rest)],
                wide.at[2 * tiles, :, pl.ds(k * rest, rest)],
                load.at[8 + 2 * tiles + k],
            )
        )
    down_load = pltpu.make_async_copy(w_down, down, load.at[10 + 2 * tiles])
    for each in weight_loads + [down_load]:
        each.start()
    greet([("ctx", sib), ("ctx", xn), ("ctx", yn)] + [("head", p) for p in zs])
    copy = sender(send, recv)

    row = lax.broadcasted_iota(jnp.int32, (128, 128), 0)
    col = lax.broadcasted_iota(jnp.int32, (128, 128), 1)
    lower = (col <= row).astype(bf16)

    def chosen(notes, expert, offset):
        e = expert.astype(f32)
        named = (notes[:, 0:1] == e) | (notes[:, 1:2] == e)
        marks = jnp.broadcast_to(named.astype(f32), (128, 128)).astype(bf16)
        slot = jnp.dot(lower, marks, preferred_element_type=f32).astype(jnp.int32) - 1 + offset
        return jnp.where((slot == col) & (marks > 0), 1.0, 0.0)

    for i in range(8):
        token_loads[i].wait()
        notes = toks[i, :, model_width:].astype(f32)
        place = chosen(notes, me, 0)
        if i >= 4:
            onehots[i - 4] = (place + chosen(notes, sib, count)).astype(bf16)
        pick = place[:, :count].astype(bf16)
        rows = lax.dot_general(
            pick, toks[i], (((0,), (0,)), ((), ())), preferred_element_type=f32
        )
        picked[i * count : (i + 1) * count] = rows[:, :model_width].astype(bf16)
        said = rows[:, model_width:]
        leading = said[:, 2:3] + said[:, 3:4] + said[:, 4:5]
        gate = jnp.where(said[:, 0:1] == me.astype(f32), leading, 1.0 - leading)
        slot_gate[i * count : (i + 1) * count] = jnp.broadcast_to(gate, (count, 128))

    def act(gated, up):
        return (gated * jax.nn.sigmoid(gated) * up).astype(bf16)

    for j in range(tiles):
        weight_loads[2 * j].wait()
        gated = jnp.dot(picked[...], wide[2 * j], preferred_element_type=f32)
        weight_loads[2 * j + 1].wait()
        up = jnp.dot(picked[...], wide[2 * j + 1], preferred_element_type=f32)
        hidden[:, j * TILE : (j + 1) * TILE] = act(gated, up)
    weight_loads[2 * tiles].wait()
    weight_loads[2 * tiles + 1].wait()
    both = jnp.dot(picked[...], wide[2 * tiles], preferred_element_type=f32)
    hidden[:, tiles * TILE :] = act(both[:, :rest], both[:, rest:])

    width = out.shape[1]
    down_load.wait()

    def project(store, first):
        rows = slice(first * count, (first + 4) * count)
        gate = slot_gate[rows, 0:1]
        for k in range(4):
            cols = slice(k * width, (k + 1) * width)
            value = jnp.dot(hidden[rows], down[:, cols], preferred_element_type=f32) * gate
            for i in range(4):
                store[i, k] = value[i * count : (i + 1) * count].astype(bf16)

    project(theirs, 0)
    pairs = [copy(PAIR + i, theirs.at[i], pair.at[i], "ctx", sib) for i in range(4)]
    for each in pairs:
        each.start()
    project(ours, 4)

    half = 64
    top, low = pl.ds(0, half), pl.ds(half, half)

    def tokens_of(i, k, rows):
        slots = jnp.concatenate([ours[i, k], pair[i, k]], axis=0)
        return jnp.dot(onehots[i, rows], slots, preferred_element_type=f32)

    plans = []
    for j in range(4):
        s = SUMS + 6 * j
        plans.append(
            [
                copy(s, ahead.at[j, 0, top], across.at[j, 0], "ctx", yn),
                copy(s + 1, ahead.at[j, 0, low], across.at[j, 1], "ctx", xn),
                copy(s + 2, ahead.at[j, 1, low], landed.at[j, 0, low], "ctx", xn),
                copy(s + 3, ahead.at[j, 2, top], landed.at[j, 1, top], "ctx", yn),
                copy(s + 4, ahead.at[j, 1, top], landed.at[j, 0, top], "ctx", xn),
                copy(s + 5, ahead.at[j, 2, low], landed.at[j, 1, low], "ctx", yn),
            ]
        )
    out_z = [
        copy(SLICES + d, total.at[d], from_z.at[d], "head", peer) for d, peer in enumerate(zs)
    ]

    def begin(j):
        k = chunks[j]
        if j == 0:
            pairs[0].wait_recv()
        ahead[j, 0] = tokens_of(0, k, slice(None)).astype(bf16)
        plans[j][0].start()
        plans[j][1].start()
        if j == 0:
            pairs[1].wait_recv()
        ahead[j, 1, low] = tokens_of(1, k, low).astype(bf16)
        plans[j][2].start()
        if j == 0:
            pairs[2].wait_recv()
        ahead[j, 2, top] = tokens_of(2, k, top).astype(bf16)
        plans[j][3].start()

    def pass_on(j):
        k = chunks[j]
        plans[j][0].wait_recv()
        ahead[j, 1, top] = (tokens_of(1, k, top) + across[j, 0].astype(f32)).astype(bf16)
        plans[j][4].start()
        plans[j][1].wait_recv()
        ahead[j, 2, low] = (tokens_of(2, k, low) + across[j, 1].astype(f32)).astype(bf16)
        plans[j][5].start()

    def finish(j):
        k = chunks[j]
        if j == 0:
            pairs[3].wait_recv()
        value = tokens_of(3, k, slice(None))
        for step in (2, 3, 4, 5):
            plans[j][step].wait_recv()
        value += landed[j, 0].astype(f32) + landed[j, 1].astype(f32)
        if j < 3:
            total[j] = value.astype(bf16)
            out_z[j].start()
        return value

    begin(0)
    begin(1)
    pass_on(0)
    begin(2)
    pass_on(1)
    finish(0)
    begin(3)
    pass_on(2)
    finish(1)
    pass_on(3)
    finish(2)
    value = finish(3) + base[...].astype(f32)
    for d in range(3):
        out_z[d].wait_recv()
        value += from_z[d].astype(f32)
    out[...] = value.astype(bf16)
    for each in pairs + sum(plans, []) + out_z:
        each.wait_send()


def run_experts(tokens, w_gate, w_up, w_down, base, capacity):
    ctx, rows, wide = tokens.shape
    model_width, units = w_gate.shape
    width = base.shape[1]
    planes = model_width // width
    dma, bf16 = pltpu.SemaphoreType.DMA, jnp.bfloat16
    tiles = units // TILE
    return pl.pallas_call(
        expert_kernel,
        out_shape=jax.ShapeDtypeStruct(base.shape, bf16),
        in_specs=[ANY] * 4 + [VMEM],
        out_specs=VMEM,
        scratch_shapes=[
            pltpu.VMEM((ctx, rows, wide), bf16),
            pltpu.VMEM((2 * tiles + 1, model_width, TILE), bf16),
            pltpu.VMEM((units, model_width), bf16),
            pltpu.VMEM((ctx * capacity, model_width), bf16),
            pltpu.VMEM((ctx * capacity, 128), jnp.float32),
            pltpu.VMEM((ctx * capacity, units), bf16),
            pltpu.VMEM((4, planes, capacity, width), bf16),
            pltpu.VMEM((4, planes, capacity, width), bf16),
            pltpu.VMEM((4, planes, capacity, width), bf16),
            pltpu.VMEM((4, rows, 2 * capacity), bf16),
            pltpu.VMEM((planes, 3, rows, width), bf16),
            pltpu.VMEM((planes, 2, rows // 2, width), bf16),
            pltpu.VMEM((planes, 2, rows, width), bf16),
            pltpu.VMEM((planes - 1, rows, width), bf16),
            pltpu.VMEM((planes - 1, rows, width), bf16),
            dma((SLICES + planes,)),
            dma((SLICES + planes,)),
            dma((11 + 2 * tiles,)),
        ],
        compiler_params=pltpu.CompilerParams(
            collective_id=3, has_side_effects=True, vmem_limit_bytes=60 << 20
        ),
        name="run_experts",
    )(tokens, w_gate, w_up, w_down, base)


def plane_body(
    query_vectors,
    key_vectors,
    value_vectors,
    log_decay,
    residual,
    out_weight,
    attn_gain,
    moe_gain,
    router,
    w_gate,
    w_up,
    w_down,
    expert_ids,
):
    token_count = query_vectors.shape[0]
    heads_here = log_decay.shape[0]
    head_size = query_vectors.shape[1] // heads_here
    ctx, planes = lax.axis_size("ctx"), lax.axis_size("head")
    me, z = lax.axis_index("ctx"), lax.axis_index("head")
    bf16, f32 = jnp.bfloat16, jnp.float32

    def split_heads(matrix_in):
        return matrix_in.astype(f32).reshape(token_count, heads_here, head_size).transpose(1, 0, 2)

    query_heads = split_heads(query_vectors)
    inside_part, running, local_state, final_log = local_attention(
        query_heads, split_heads(key_vectors), split_heads(value_vectors), log_decay
    )
    logs = jnp.broadcast_to(final_log[:, None], (heads_here, head_size))
    states, all_logs = plane_gather(
        1,
        local_state.astype(bf16).reshape(heads_here * head_size, head_size),
        jnp.concatenate([logs, jnp.zeros_like(logs)], axis=0),
    )
    all_logs = all_logs[:, :heads_here, 0]
    place = lax.broadcasted_iota(jnp.int32, (ctx, 1), 0)
    before = place < me
    later = jnp.where(before, all_logs, 0.0)
    after = jnp.cumsum(later[::-1], axis=0)[::-1] - later
    scale = jnp.where(before, jnp.exp(after), 0.0)
    prior_state = jnp.sum(
        scale[:, :, None, None]
        * states.reshape(ctx, heads_here, head_size, head_size).astype(f32),
        axis=0,
    )
    outside_part = jnp.exp(running)[:, :, None] * jnp.einsum(
        "htd,hde->hte", query_heads, prior_state, precision=PRECISE
    )
    attended = inside_part + outside_part
    square_mean = jnp.mean(attended * attended, axis=2, keepdims=True)
    heads_normed = (
        attended * lax.rsqrt(square_mean + 1e-05) * attn_gain.reshape(heads_here, 1, head_size)
    )
    heads_normed = (
        heads_normed.astype(bf16).transpose(1, 0, 2).reshape(token_count, heads_here * head_size)
    )
    share = token_count // planes
    base, tokens = spread_rows(
        heads_normed,
        out_weight,
        lax.dynamic_slice_in_dim(residual, z * share, share, 0),
        moe_gain[None, :],
        router.T,
        lax.dynamic_slice_in_dim(expert_ids, z * share, share, 0),
    )
    return run_experts(
        tokens.reshape(ctx, token_count, tokens.shape[-1]),
        w_gate[0],
        w_up[0],
        w_down[0],
        base.reshape(token_count, -1),
        2 * token_count * TOP // router.shape[1],
    )


def solution(mesh):
    sizes = dict(mesh.shape)
    body = plane_body if (sizes["ctx"], sizes["head"]) == (8, 4) else general_body
    in_specs = (
        P("ctx", "head"),
        P("ctx", "head"),
        P("ctx", "head"),
        P("head", "ctx"),
        P("ctx", None),
        P("head", "ctx"),
        P("head"),
        P(),
        P(),
        P("ctx", None, "head"),
        P("ctx", None, "head"),
        P("ctx", "head", None),
        P("ctx", None),
    )
    out_specs = P("ctx", "head")
    return jax.shard_map(body, mesh=mesh, in_specs=in_specs, out_specs=out_specs, check_vma=False)
```

```python
import functools

import jax
import jax.numpy as jnp
from jax import lax
from jax.experimental import pallas as pl
from jax.experimental.pallas import tpu as pltpu
from jax.sharding import PartitionSpec as P

TOP = 2


PRECISE = lax.Precision.HIGHEST


def entering(value, axis, combine, identity):
    peers, index = (lax.axis_size(axis), lax.axis_index(axis))
    everything = jax.tree.map(
        lambda part, kind: lax.all_gather(part.astype(kind), axis),
        value,
        (jnp.bfloat16, jnp.bfloat16),
    )
    start = jax.tree.map(
        lambda part, zero: jnp.broadcast_to(jnp.asarray(zero, part.dtype), part.shape),
        value,
        identity,
    )

    def step(k, before):
        reached = k < index
        new = combine(
            before, jax.tree.map(lambda part, own: part[k].astype(own.dtype), everything, value)
        )
        return jax.tree.map(lambda a, b: jnp.where(reached, a, b), new, before)

    return lax.fori_loop(0, peers, step, start)


def local_attention(query_block, key_block, value_block, decay_block):
    running = jnp.cumsum(decay_block, axis=1)
    length_here = decay_block.shape[1]
    row_index = lax.broadcasted_iota(jnp.int32, (length_here, length_here), 0)
    col_index = lax.broadcasted_iota(jnp.int32, (length_here, length_here), 1)
    causal = (col_index <= row_index)[None]
    spread = jnp.where(causal, running[:, :, None] - running[:, None, :], 0.0)
    decay_weights = jnp.where(causal, jnp.exp(spread), 0.0)
    scores = jnp.einsum("htd,hsd->hts", query_block, key_block, precision=PRECISE) * decay_weights
    inside_part = jnp.einsum("hts,hse->hte", scores, value_block, precision=PRECISE)
    final_log = running[:, -1]
    tail_decay = jnp.exp(final_log[:, None] - running)
    local_state = jnp.einsum(
        "hsd,hse->hde", key_block * tail_decay[:, :, None], value_block, precision=PRECISE
    )
    return (inside_part, running, local_state, final_log)


def route_tokens(logits, expert_ids, experts_total):
    onehot = expert_ids[:, :, None] == lax.broadcasted_iota(jnp.int32, (1, 1, experts_total), 2)
    chosen = jnp.sum(jnp.where(onehot, logits[:, None, :], 0.0), axis=2)
    leading = jax.nn.sigmoid(chosen[:, 0] - chosen[:, 1])
    gate_weights = jnp.stack([leading, 1.0 - leading], axis=1)
    marked = onehot.reshape(-1, experts_total).astype(jnp.int32)
    earlier = jnp.cumsum(marked, axis=0) - marked
    slot_index = jnp.sum(earlier * marked, axis=1).reshape(expert_ids.shape)
    return (gate_weights, slot_index)


def link_states(earlier, later):
    return (earlier[0] + later[0], jnp.exp(later[0])[:, None, None] * earlier[1] + later[1])


def general_body(
    query_vectors,
    key_vectors,
    value_vectors,
    log_decay,
    residual,
    out_weight,
    attn_gain,
    moe_gain,
    router,
    w_gate,
    w_up,
    w_down,
    expert_ids,
):
    token_count = query_vectors.shape[0]
    heads_here = log_decay.shape[0]
    head_size = query_vectors.shape[1] // heads_here

    def split_heads(matrix_in):
        return (
            matrix_in.astype(jnp.float32)
            .reshape(token_count, heads_here, head_size)
            .transpose(1, 0, 2)
        )

    query_heads = split_heads(query_vectors)
    inside_part, running, local_state, final_log = local_attention(
        query_heads, split_heads(key_vectors), split_heads(value_vectors), log_decay
    )
    identity = (jnp.zeros_like(final_log), jnp.zeros_like(local_state))
    _, prior_state = entering((final_log, local_state), "ctx", link_states, identity)
    outside_part = jnp.exp(running)[:, :, None] * jnp.einsum(
        "htd,hde->hte", query_heads, prior_state, precision=PRECISE
    )
    attended = inside_part + outside_part
    square_mean = jnp.mean(attended * attended, axis=2, keepdims=True)
    heads_normed = (
        attended * lax.rsqrt(square_mean + 1e-05) * attn_gain.reshape(heads_here, 1, head_size)
    )
    heads_normed = (
        heads_normed.astype(jnp.bfloat16)
        .transpose(1, 0, 2)
        .reshape(token_count, heads_here * head_size)
    )
    partial_out = jnp.dot(
        heads_normed,
        lax.all_gather(out_weight, "ctx", axis=1, tiled=True),
        preferred_element_type=jnp.float32,
    )
    model_width = residual.shape[1]
    experts_total = router.shape[1]
    capacity = 2 * token_count * TOP // experts_total
    slice_width = model_width // lax.axis_size("head")
    slice_start = lax.axis_index("head") * slice_width
    projected = lax.psum(partial_out.astype(jnp.bfloat16), "head").astype(jnp.float32)
    mixed_rows = (residual.astype(jnp.float32) + projected).astype(jnp.bfloat16)
    mixed_wide = mixed_rows.astype(jnp.float32)
    inv_rms = lax.rsqrt(jnp.mean(mixed_wide * mixed_wide, axis=1, keepdims=True) + 1e-06)
    scaled = mixed_wide * moe_gain[None, :]
    moe_in = (scaled * inv_rms).astype(jnp.bfloat16)
    logits = inv_rms * jnp.dot(scaled, router, precision=PRECISE)
    base_slice = lax.dynamic_slice_in_dim(mixed_wide, slice_start, slice_width, 1)
    gate_weights, slot_index = route_tokens(logits, expert_ids, experts_total)
    target = (expert_ids * capacity + slot_index).reshape(-1)
    width_here = moe_in.shape[1]
    source = jnp.repeat(moe_in, TOP, axis=0)
    packed = jnp.zeros((experts_total * capacity, width_here), jnp.bfloat16).at[target].set(source)
    arrived = lax.all_to_all(
        packed.reshape(experts_total, capacity, width_here),
        "ctx",
        split_axis=0,
        concat_axis=0,
        tiled=True,
    )
    flat_rows = arrived.reshape(-1, model_width)
    gate_part = jnp.dot(flat_rows, w_gate[0], preferred_element_type=jnp.float32)
    up_part = jnp.dot(flat_rows, w_up[0], preferred_element_type=jnp.float32)
    hidden = (jax.nn.silu(gate_part) * up_part).astype(jnp.bfloat16)
    partial_down = jnp.dot(hidden, w_down[0], preferred_element_type=jnp.float32).reshape(
        arrived.shape
    )
    returned = lax.all_to_all(
        lax.all_to_all(
            partial_down.astype(jnp.bfloat16)[None], "ctx", split_axis=1, concat_axis=1, tiled=True
        ),
        "head",
        split_axis=3,
        concat_axis=0,
        tiled=True,
    )
    expert_out = jnp.sum(returned.astype(jnp.float32), axis=0).astype(jnp.bfloat16)
    lookup = expert_out.reshape(experts_total * capacity, slice_width)
    picked = lookup[target].reshape(token_count, TOP, slice_width).astype(jnp.float32)
    final_out = (
        base_slice + gate_weights[:, 0:1] * picked[:, 0] + gate_weights[:, 1:2] * picked[:, 1]
    )
    return final_out.astype(jnp.bfloat16)


MESH = pl.DeviceIdType.MESH
ANY = pl.BlockSpec(memory_space=pl.ANY)
VMEM = pl.BlockSpec(memory_space=pltpu.VMEM)


def plane_peers():
    me = lax.axis_index("ctx")
    core, x, y = me % 2, (me // 2) % 2, me // 4

    def at(c, a, b):
        return (b * 2 + a) * 2 + c

    return (
        me,
        at(1 - core, x, y),
        at(core, 1 - x, y),
        at(core, x, 1 - y),
        at(core, 1 - x, 1 - y),
    )


def greet(axes_and_peers):
    barrier = pltpu.get_barrier_semaphore()
    for axis, peer in axes_and_peers:
        pl.semaphore_signal(barrier, inc=1, device_id={axis: peer}, device_id_type=MESH)
    pl.semaphore_wait(barrier, len(axes_and_peers))


def block_order(me, sib, xn, yn, dg):
    def other_core(index):
        return index + 1 - 2 * (index % 2)

    return (me, sib, xn, yn, other_core(xn), other_core(yn), dg, other_core(dg))


def z_order():
    z = lax.axis_index("head")
    return (z + 1 - 2 * (z % 2), z + 2 - 4 * (z // 2), 3 - z)


def sender(send, recv):
    def copy(at, src, dst, axis, peer):
        return pltpu.make_async_remote_copy(
            src_ref=src,
            dst_ref=dst,
            send_sem=send.at[at],
            recv_sem=recv.at[at],
            device_id={axis: peer},
            device_id_type=MESH,
        )

    return copy


STATES, GATHER, TO_Z, TO_COLS = 0, 9, 18, 42
ROWS_Z, BASE_Z, SPREAD, PAIR, SUMS, SLICES, COPIES = 50, 53, 56, 92, 96, 120, 123
TILE = 256


def gather_plan(copy, first, buffer, split, peers):
    me, sib, xn, yn, dg = peers
    top, low = pl.ds(0, split), pl.ds(split, buffer.shape[1] - split)
    return [
        copy(first, buffer.at[me], buffer.at[me], "ctx", sib),
        copy(first + 1, buffer.at[me], buffer.at[me], "ctx", xn),
        copy(first + 2, buffer.at[me], buffer.at[me], "ctx", yn),
        copy(first + 3, buffer.at[xn, top], buffer.at[xn, top], "ctx", yn),
        copy(first + 4, buffer.at[xn], buffer.at[xn], "ctx", sib),
        copy(first + 5, buffer.at[yn, low], buffer.at[yn, low], "ctx", xn),
        copy(first + 6, buffer.at[yn], buffer.at[yn], "ctx", sib),
        copy(first + 7, buffer.at[dg, top], buffer.at[dg, top], "ctx", sib),
        copy(first + 8, buffer.at[dg, low], buffer.at[dg, low], "ctx", sib),
    ]


def attend(query, key, value, log_decay, attn_gain, states, rows, copy, peers):
    f32, bf16 = jnp.float32, jnp.bfloat16
    me = peers[0]
    heads, length = log_decay.shape
    size = query.shape[1] // heads
    row = lax.broadcasted_iota(jnp.int32, (length, length), 0)
    col = lax.broadcasted_iota(jnp.int32, (length, length), 1)
    causal = col <= row
    lower = causal.astype(f32)
    decay = log_decay[...]
    across = (((1,), (1,)), ((), ()))
    by_row = lax.dot_general(
        decay, lower, across, precision=PRECISE, preferred_element_type=f32
    )
    by_col = lax.dot_general(
        lower, decay, across, precision=PRECISE, preferred_element_type=f32
    )
    final = by_row[:, length - 1 :]
    for h in range(heads):
        cols = slice(h * size, (h + 1) * size)
        tail = jnp.exp(by_col[length - 1 :, h : h + 1] - by_col[:, h : h + 1])
        state = lax.dot_general(
            (key[:, cols].astype(f32) * tail).astype(bf16),
            value[:, cols],
            (((0,), (0,)), ((), ())),
            preferred_element_type=f32,
        )
        states[me, h * size : (h + 1) * size] = state.astype(bf16)
    big = final.astype(bf16).astype(f32)
    middle = (final - big).astype(bf16).astype(f32)
    small = final - big - middle
    lane = lax.broadcasted_iota(jnp.int32, (heads, size), 1)
    notes = jnp.zeros((heads, size), f32)
    for k, term in enumerate((big, middle, small)):
        notes = jnp.where(lane == k, term, notes)
    notes = jnp.concatenate([notes, jnp.zeros((16 - heads, size), f32)], axis=0)
    states[me, heads * size :] = notes.astype(bf16)

    plan = gather_plan(copy, STATES, states, heads * size // 2, peers)
    for step in (1, 2, 0):
        plan[step].start()
    inside = []
    for h in range(heads):
        cols = slice(h * size, (h + 1) * size)
        scores = lax.dot_general(
            query[:, cols], key[:, cols], across, preferred_element_type=f32
        )
        spread = jnp.where(causal, by_col[:, h : h + 1] - by_row[h : h + 1], 0.0)
        scores *= jnp.where(causal, jnp.exp(spread), 0.0)
        inside.append(
            jnp.dot(scores.astype(bf16), value[:, cols], preferred_element_type=f32)
        )
    for got, onward in ((1, (3, 4)), (2, (5, 6)), (3, (7,)), (5, (8,))):
        plan[got].wait_recv()
        for step in onward:
            plan[step].start()
    for step in (0, 4, 6, 7, 8):
        plan[step].wait_recv()

    scales = [None] * states.shape[0]
    after = jnp.zeros((heads, 1), f32)
    for k in reversed(range(states.shape[0])):
        said = states[k, heads * size :].astype(f32)[:heads]
        scales[k] = jnp.where(k < me, jnp.exp(after), 0.0)
        after += jnp.where(k < me, said[:, 0:1] + said[:, 1:2] + said[:, 2:3], 0.0)
    for h in range(heads):
        cols = slice(h * size, (h + 1) * size)
        prior = jnp.zeros((size, size), f32)
        for k in range(states.shape[0]):
            prior += scales[k][h : h + 1] * states[k, h * size : (h + 1) * size].astype(f32)
        outside = jnp.dot(query[:, cols], prior.astype(bf16), preferred_element_type=f32)
        attended = inside[h] + jnp.exp(by_col[:, h : h + 1]) * outside
        square_mean = jnp.mean(attended * attended, axis=1, keepdims=True)
        normed = attended * lax.rsqrt(square_mean + 1e-05) * attn_gain[:, cols]
        rows[me, :, cols] = normed.astype(bf16)
    return plan


def layer_kernel(
    query, key, value, log_decay, attn_gain, weight, residual, gain, router, ids,
    w_gate, w_up, w_down, out,
    states, rows, part, from_z, summed, by_cols, mixed, base, toks,
    wide, down, picked, slot_gate, hidden, theirs, ours, pair, onehots,
    ahead, across, landed, total, slices, send, recv, load,
):
    peers = plane_peers()
    me, sib, xn, yn, dg = peers
    z = lax.axis_index("head")
    blocks, zs = block_order(*peers), z_order()
    chunks = zs + (z,)
    units = hidden.shape[1]
    tiles = units // TILE
    weight_loads = []
    for j in range(tiles):
        for k, matrix in enumerate((w_gate, w_up)):
            weight_loads.append(
                pltpu.make_async_copy(
                    matrix.at[:, pl.ds(j * TILE, TILE)],
                    wide.at[2 * j + k],
                    load.at[2 * j + k],
                )
            )
    rest = units - tiles * TILE
    for k, matrix in enumerate((w_gate, w_up)):
        weight_loads.append(
            pltpu.make_async_copy(
                matrix.at[:, pl.ds(tiles * TILE, rest)],
                wide.at[2 * tiles, :, pl.ds(k * rest, rest)],
                load.at[2 * tiles + k],
            )
        )
    down_load = pltpu.make_async_copy(w_down, down, load.at[2 + 2 * tiles])
    for each in weight_loads + [down_load]:
        each.start()
    greet([("ctx", b) for b in blocks[1:]] + [("head", p) for p in zs])
    copy = sender(send, recv)
    f32, bf16 = jnp.float32, jnp.bfloat16
    share, model_width = residual.shape
    mine = pl.ds(pl.multiple_of(z * share, share), share)
    width = weight.shape[1]

    sent = attend(
        query, key, value, log_decay, attn_gain, states, rows, copy, peers
    )
    plan = gather_plan(copy, GATHER, rows, rows.shape[1] // 2, peers)
    for step in (1, 2, 0):
        plan[step].start()
    sent = sent + plan
    z_in = []

    def project(i, block):
        product = jnp.dot(block, weight[...], preferred_element_type=f32).astype(bf16)
        for k in range(len(zs) + 1):
            part[i, k] = product[k * share : (k + 1) * share]
        z_in.append([])
        for d, peer in enumerate(zs):
            out_copy = copy(
                TO_Z + 3 * i + d, part.at[i, peer], from_z.at[i, d], "head", peer
            )
            out_copy.start()
            z_in[i].append(out_copy)
            sent.append(out_copy)

    def arrived(*steps):
        for step in steps:
            plan[step].wait_recv()

    project(0, rows[me])
    arrived(0)
    project(1, rows[sib])
    arrived(1)
    plan[3].start()
    plan[4].start()
    project(2, rows[xn])
    arrived(2)
    plan[5].start()
    plan[6].start()
    project(3, rows[yn])
    arrived(4)
    project(4, rows[blocks[4]])
    arrived(6)
    project(5, rows[blocks[5]])
    arrived(3)
    plan[7].start()
    arrived(5)
    plan[8].start()
    project(6, rows[dg])
    arrived(7, 8)
    project(7, rows[blocks[7]])

    col_copies = []
    for i, block in enumerate(blocks):
        block_sum = part[i, z].astype(f32)
        for d in range(3):
            z_in[i][d].wait_recv()
            block_sum += from_z[i, d].astype(f32)
        summed[i] = block_sum.astype(bf16)
        if i:
            col_copies.append(
                copy(TO_COLS + i, summed.at[i], by_cols.at[me], "ctx", block)
            )
            col_copies[-1].start()
    by_cols[me] = summed[0]
    for each in col_copies:
        each.wait_recv()
    sent += col_copies

    per = model_width // (len(zs) + 1) // width
    squares = jnp.zeros((share, 1), f32)
    for k in range(model_width // width):
        cols = slice(k * width, (k + 1) * width)
        whole = (residual[:, cols].astype(f32) + by_cols[k].astype(f32)).astype(bf16)
        mixed[k // per, :, (k % per) * width : (k % per + 1) * width] = whole
        row_values = whole.astype(f32)
        squares += jnp.sum(row_values * row_values, axis=1, keepdims=True)
    inv_rms = lax.rsqrt(squares / model_width + 1e-06)
    experts_total = router.shape[0]
    logits = [jnp.zeros((share, 1), f32)] * experts_total
    slice_width = per * width
    for k in range(len(zs) + 1):
        cols = slice(k * slice_width, (k + 1) * slice_width)
        scaled = mixed[k].astype(f32) * gain[:, cols]
        toks[me, mine, cols] = (scaled * inv_rms).astype(bf16)
        for e in range(experts_total):
            logits[e] += jnp.sum(scaled * router[e : e + 1, cols], axis=1, keepdims=True)
    first, second = ids[:, 0:1], ids[:, 1:2]
    margin = jnp.zeros((share, 1), f32)
    for e in range(experts_total):
        margin += jnp.where(first == e, logits[e], 0.0) - jnp.where(second == e, logits[e], 0.0)
    leading = jax.nn.sigmoid(margin * inv_rms)
    big = leading.astype(bf16).astype(f32)
    middle = (leading - big).astype(bf16).astype(f32)
    small = leading - big - middle
    lane = lax.broadcasted_iota(jnp.int32, (share, 128), 1)
    notes = jnp.zeros((share, 128), f32)
    for k, value in enumerate((first.astype(f32), second.astype(f32), big, middle, small)):
        notes = jnp.where(lane == k, value, notes)
    toks[me, mine, model_width:] = notes.astype(bf16)
    base[mine] = mixed[z]

    z_copies, base_copies = [], []
    quarter = share // 2

    def spread(j, k):
        s = SPREAD + 9 * j
        start = pl.multiple_of(k * share, share)
        rows_of = pl.ds(start, share)
        upper, lower = pl.ds(start, quarter), pl.ds(start + quarter, quarter)

        def send_on(step, block, part_of, peer):
            ref = toks.at[block, part_of]
            return copy(s + step, ref, ref, "ctx", peer)

        steps = [
            send_on(0, me, rows_of, sib),
            send_on(1, me, rows_of, xn),
            send_on(2, me, rows_of, yn),
            send_on(3, xn, upper, yn),
            send_on(4, xn, rows_of, sib),
            send_on(5, yn, lower, xn),
            send_on(6, yn, rows_of, sib),
            send_on(7, dg, upper, sib),
            send_on(8, dg, lower, sib),
        ]
        for step in (1, 2, 0):
            steps[step].start()
        return steps

    def relay(steps):
        for got, onward in ((1, (3, 4)), (2, (5, 6)), (3, (7,)), (5, (8,))):
            steps[got].wait_recv()
            for step in onward:
                steps[step].start()

    for d, peer in enumerate(zs):
        z_copies.append(
            copy(ROWS_Z + d, toks.at[me, mine], toks.at[me, mine], "head", peer)
        )
        z_copies[-1].start()
    runs = [spread(0, z)]
    for d, peer in enumerate(zs):
        z_copies[d].wait_recv()
        runs.append(spread(d + 1, peer))
        relay(runs[d])
    for d, peer in enumerate(zs):
        base_copies.append(copy(BASE_Z + d, mixed.at[peer], base.at[mine], "head", peer))
        base_copies[-1].start()
    relay(runs[3])
    for steps in runs:
        for step in (0, 4, 6, 7, 8):
            steps[step].wait_recv()
        sent += steps
    for each in base_copies:
        each.wait_recv()
    sent += z_copies + base_copies

    count = picked.shape[0] // 4
    row = lax.broadcasted_iota(jnp.int32, (128, 128), 0)
    col = lax.broadcasted_iota(jnp.int32, (128, 128), 1)
    lower = (col <= row).astype(bf16)

    def chosen(notes, expert, offset):
        e = expert.astype(f32)
        named = (notes[:, 0:1] == e) | (notes[:, 1:2] == e)
        marks = jnp.broadcast_to(named.astype(f32), (128, 128)).astype(bf16)
        slot = jnp.dot(lower, marks, preferred_element_type=f32).astype(jnp.int32) - 1 + offset
        return jnp.where((slot == col) & (marks > 0), 1.0, 0.0)

    width = out.shape[1]
    away = (blocks[7], blocks[4], blocks[5], sib)
    here = (dg, xn, yn, me)
    pairs = [copy(PAIR + i, theirs.at[i], pair.at[i], "ctx", sib) for i in range(4)]

    def act(gated, up):
        return (gated * jax.nn.sigmoid(gated) * up).astype(bf16)

    def experts(group):
        both = (2 * group, 2 * group + 1)
        for n, block in enumerate([away[i] for i in both] + [here[i] for i in both]):
            notes = toks[block, :, model_width:].astype(f32)
            place = chosen(notes, me, 0)
            if n >= 2:
                onehots[both[n - 2]] = (place + chosen(notes, sib, count)).astype(bf16)
            pick = place[:, :count].astype(bf16)
            found = lax.dot_general(
                pick, toks[block], (((0,), (0,)), ((), ())), preferred_element_type=f32
            )
            picked[n * count : (n + 1) * count] = found[:, :model_width].astype(bf16)
            said = found[:, model_width:]
            leading = said[:, 2:3] + said[:, 3:4] + said[:, 4:5]
            gate = jnp.where(said[:, 0:1] == me.astype(f32), leading, 1.0 - leading)
            slot_gate[n * count : (n + 1) * count] = jnp.broadcast_to(gate, (count, 128))
        for j in range(tiles):
            if group == 0:
                weight_loads[2 * j].wait()
                weight_loads[2 * j + 1].wait()
            gated = jnp.dot(picked[...], wide[2 * j], preferred_element_type=f32)
            up = jnp.dot(picked[...], wide[2 * j + 1], preferred_element_type=f32)
            hidden[:, j * TILE : (j + 1) * TILE] = act(gated, up)
        if group == 0:
            weight_loads[2 * tiles].wait()
            weight_loads[2 * tiles + 1].wait()
            down_load.wait()
        last = jnp.dot(picked[...], wide[2 * tiles], preferred_element_type=f32)
        hidden[:, tiles * TILE :] = act(last[:, :rest], last[:, rest:])
        for k in range(4):
            cols = slice(k * width, (k + 1) * width)
            result = jnp.dot(hidden[...], down[:, cols], preferred_element_type=f32)
            result = (result * slot_gate[:, 0:1]).astype(bf16)
            for n in range(2):
                theirs[both[n], k] = result[n * count : (n + 1) * count]
                ours[both[n], k] = result[(n + 2) * count : (n + 3) * count]
        for i in both:
            pairs[i].start()

    half = 64
    top, low = pl.ds(0, half), pl.ds(half, half)

    def tokens_of(i, k, rows):
        slots = jnp.concatenate([ours[i, k], pair[i, k]], axis=0)
        return jnp.dot(onehots[i, rows], slots, preferred_element_type=f32)

    plans = []
    for j in range(4):
        s = SUMS + 6 * j
        plans.append(
            [
                copy(s, ahead.at[j, 0, top], across.at[j, 0], "ctx", yn),
                copy(s + 1, ahead.at[j, 0, low], across.at[j, 1], "ctx", xn),
                copy(s + 2, ahead.at[j, 1, low], landed.at[j, 0, low], "ctx", xn),
                copy(s + 3, ahead.at[j, 2, top], landed.at[j, 1, top], "ctx", yn),
                copy(s + 4, ahead.at[j, 1, top], landed.at[j, 0, top], "ctx", xn),
                copy(s + 5, ahead.at[j, 2, low], landed.at[j, 1, low], "ctx", yn),
            ]
        )
    out_z = [
        copy(SLICES + d, total.at[d], slices.at[d], "head", peer) for d, peer in enumerate(zs)
    ]

    def begin(j):
        k = chunks[j]
        ahead[j, 0] = tokens_of(0, k, slice(None)).astype(bf16)
        plans[j][0].start()
        plans[j][1].start()
        ahead[j, 1, low] = tokens_of(1, k, low).astype(bf16)
        plans[j][2].start()

    def begin_y(j):
        ahead[j, 2, top] = tokens_of(2, chunks[j], top).astype(bf16)
        plans[j][3].start()

    def pass_on(j):
        k = chunks[j]
        plans[j][0].wait_recv()
        ahead[j, 1, top] = (tokens_of(1, k, top) + across[j, 0].astype(f32)).astype(bf16)
        plans[j][4].start()
        plans[j][1].wait_recv()
        ahead[j, 2, low] = (tokens_of(2, k, low) + across[j, 1].astype(f32)).astype(bf16)
        plans[j][5].start()

    def finish(j):
        k = chunks[j]
        value = tokens_of(3, k, slice(None))
        for step in (2, 3, 4, 5):
            plans[j][step].wait_recv()
        value += landed[j, 0].astype(f32) + landed[j, 1].astype(f32)
        if j < 3:
            total[j] = value.astype(bf16)
            out_z[j].start()
        return value

    experts(0)
    pairs[0].wait_recv()
    pairs[1].wait_recv()
    for j in range(4):
        begin(j)
    experts(1)
    pairs[2].wait_recv()
    begin_y(0)
    begin_y(1)
    pass_on(0)
    begin_y(2)
    pass_on(1)
    pairs[3].wait_recv()
    finish(0)
    begin_y(3)
    pass_on(2)
    finish(1)
    pass_on(3)
    finish(2)
    value = finish(3) + base[...].astype(f32)
    for d in range(3):
        out_z[d].wait_recv()
        value += slices[d].astype(f32)
    out[...] = value.astype(bf16)
    for each in sent + pairs + sum(plans, []) + out_z:
        each.wait_send()


def layer(tensors, weights, capacity):
    ctx, planes = lax.axis_size("ctx"), lax.axis_size("head")
    query, decay, weight, residual = tensors[0], tensors[3], tensors[5], tensors[6]
    tokens, depth = query.shape
    width = weight.shape[1]
    share, model_width = residual.shape
    units = weights[0].shape[1]
    part_width = model_width // planes
    tiles = units // TILE
    dma, bf16 = pltpu.SemaphoreType.DMA, jnp.bfloat16
    return pl.pallas_call(
        layer_kernel,
        out_shape=jax.ShapeDtypeStruct((tokens, part_width), bf16),
        in_specs=[VMEM] * len(tensors) + [ANY] * len(weights),
        out_specs=VMEM,
        scratch_shapes=[
            pltpu.VMEM((ctx, depth + 16, depth // decay.shape[0]), bf16),
            pltpu.VMEM((ctx, tokens, depth), bf16),
            pltpu.VMEM((ctx, planes, share, width), bf16),
            pltpu.VMEM((ctx, planes - 1, share, width), bf16),
            pltpu.VMEM((ctx, share, width), bf16),
            pltpu.VMEM((ctx, share, width), bf16),
            pltpu.VMEM((planes, share, part_width), bf16),
            pltpu.VMEM((tokens, part_width), bf16),
            pltpu.VMEM((ctx, tokens, model_width + 128), bf16),
            pltpu.VMEM((2 * tiles + 1, model_width, TILE), bf16),
            pltpu.VMEM((units, model_width), bf16),
            pltpu.VMEM((ctx // 2 * capacity, model_width), bf16),
            pltpu.VMEM((ctx // 2 * capacity, 128), jnp.float32),
            pltpu.VMEM((ctx // 2 * capacity, units), bf16),
            pltpu.VMEM((4, planes, capacity, part_width), bf16),
            pltpu.VMEM((4, planes, capacity, part_width), bf16),
            pltpu.VMEM((4, planes, capacity, part_width), bf16),
            pltpu.VMEM((4, tokens, 2 * capacity), bf16),
            pltpu.VMEM((planes, 3, tokens, part_width), bf16),
            pltpu.VMEM((planes, 2, tokens // 2, part_width), bf16),
            pltpu.VMEM((planes, 2, tokens, part_width), bf16),
            pltpu.VMEM((planes - 1, tokens, part_width), bf16),
            pltpu.VMEM((planes - 1, tokens, part_width), bf16),
            dma((COPIES,)),
            dma((COPIES,)),
            dma((3 + 2 * tiles,)),
        ],
        compiler_params=pltpu.CompilerParams(
            collective_id=1, has_side_effects=True, vmem_limit_bytes=62 << 20
        ),
        name="layer",
    )(*tensors, *weights)


def plane_body(
    query_vectors,
    key_vectors,
    value_vectors,
    log_decay,
    residual,
    out_weight,
    attn_gain,
    moe_gain,
    router,
    w_gate,
    w_up,
    w_down,
    expert_ids,
):
    token_count = query_vectors.shape[0]
    z, planes = lax.axis_index("head"), lax.axis_size("head")
    share = token_count // planes
    tensors = (
        query_vectors,
        key_vectors,
        value_vectors,
        log_decay,
        attn_gain[None, :],
        out_weight,
        lax.dynamic_slice_in_dim(residual, z * share, share, 0),
        moe_gain[None, :],
        router.T,
        lax.dynamic_slice_in_dim(expert_ids, z * share, share, 0),
    )
    capacity = 2 * token_count * TOP // router.shape[1]
    return layer(tensors, (w_gate[0], w_up[0], w_down[0]), capacity)


def solution(mesh):
    sizes = dict(mesh.shape)
    body = plane_body if (sizes["ctx"], sizes["head"]) == (8, 4) else general_body
    in_specs = (
        P("ctx", "head"),
        P("ctx", "head"),
        P("ctx", "head"),
        P("head", "ctx"),
        P("ctx", None),
        P("head", "ctx"),
        P("head"),
        P(),
        P(),
        P("ctx", None, "head"),
        P("ctx", None, "head"),
        P("ctx", "head", None),
        P("ctx", None),
    )
    out_specs = P("ctx", "head")
    return jax.shard_map(body, mesh=mesh, in_specs=in_specs, out_specs=out_specs, check_vma=False)
```

```python
import functools

import jax
import jax.numpy as jnp
from jax import lax
from jax.experimental import pallas as pl
from jax.experimental.pallas import tpu as pltpu
from jax.sharding import PartitionSpec as P

TOP = 2


PRECISE = lax.Precision.HIGHEST


def entering(value, axis, combine, identity):
    peers, index = (lax.axis_size(axis), lax.axis_index(axis))
    everything = jax.tree.map(
        lambda part, kind: lax.all_gather(part.astype(kind), axis),
        value,
        (jnp.bfloat16, jnp.bfloat16),
    )
    start = jax.tree.map(
        lambda part, zero: jnp.broadcast_to(jnp.asarray(zero, part.dtype), part.shape),
        value,
        identity,
    )

    def step(k, before):
        reached = k < index
        new = combine(
            before, jax.tree.map(lambda part, own: part[k].astype(own.dtype), everything, value)
        )
        return jax.tree.map(lambda a, b: jnp.where(reached, a, b), new, before)

    return lax.fori_loop(0, peers, step, start)


def local_attention(query_block, key_block, value_block, decay_block):
    running = jnp.cumsum(decay_block, axis=1)
    length_here = decay_block.shape[1]
    row_index = lax.broadcasted_iota(jnp.int32, (length_here, length_here), 0)
    col_index = lax.broadcasted_iota(jnp.int32, (length_here, length_here), 1)
    causal = (col_index <= row_index)[None]
    spread = jnp.where(causal, running[:, :, None] - running[:, None, :], 0.0)
    decay_weights = jnp.where(causal, jnp.exp(spread), 0.0)
    scores = jnp.einsum("htd,hsd->hts", query_block, key_block, precision=PRECISE) * decay_weights
    inside_part = jnp.einsum("hts,hse->hte", scores, value_block, precision=PRECISE)
    final_log = running[:, -1]
    tail_decay = jnp.exp(final_log[:, None] - running)
    local_state = jnp.einsum(
        "hsd,hse->hde", key_block * tail_decay[:, :, None], value_block, precision=PRECISE
    )
    return (inside_part, running, local_state, final_log)


def route_tokens(logits, expert_ids, experts_total):
    onehot = expert_ids[:, :, None] == lax.broadcasted_iota(jnp.int32, (1, 1, experts_total), 2)
    chosen = jnp.sum(jnp.where(onehot, logits[:, None, :], 0.0), axis=2)
    leading = jax.nn.sigmoid(chosen[:, 0] - chosen[:, 1])
    gate_weights = jnp.stack([leading, 1.0 - leading], axis=1)
    marked = onehot.reshape(-1, experts_total).astype(jnp.int32)
    earlier = jnp.cumsum(marked, axis=0) - marked
    slot_index = jnp.sum(earlier * marked, axis=1).reshape(expert_ids.shape)
    return (gate_weights, slot_index)


def link_states(earlier, later):
    return (earlier[0] + later[0], jnp.exp(later[0])[:, None, None] * earlier[1] + later[1])


def general_body(
    query_vectors,
    key_vectors,
    value_vectors,
    log_decay,
    residual,
    out_weight,
    attn_gain,
    moe_gain,
    router,
    w_gate,
    w_up,
    w_down,
    expert_ids,
):
    token_count = query_vectors.shape[0]
    heads_here = log_decay.shape[0]
    head_size = query_vectors.shape[1] // heads_here

    def split_heads(matrix_in):
        return (
            matrix_in.astype(jnp.float32)
            .reshape(token_count, heads_here, head_size)
            .transpose(1, 0, 2)
        )

    query_heads = split_heads(query_vectors)
    inside_part, running, local_state, final_log = local_attention(
        query_heads, split_heads(key_vectors), split_heads(value_vectors), log_decay
    )
    identity = (jnp.zeros_like(final_log), jnp.zeros_like(local_state))
    _, prior_state = entering((final_log, local_state), "ctx", link_states, identity)
    outside_part = jnp.exp(running)[:, :, None] * jnp.einsum(
        "htd,hde->hte", query_heads, prior_state, precision=PRECISE
    )
    attended = inside_part + outside_part
    square_mean = jnp.mean(attended * attended, axis=2, keepdims=True)
    heads_normed = (
        attended * lax.rsqrt(square_mean + 1e-05) * attn_gain.reshape(heads_here, 1, head_size)
    )
    heads_normed = (
        heads_normed.astype(jnp.bfloat16)
        .transpose(1, 0, 2)
        .reshape(token_count, heads_here * head_size)
    )
    partial_out = jnp.dot(
        heads_normed,
        lax.all_gather(out_weight, "ctx", axis=1, tiled=True),
        preferred_element_type=jnp.float32,
    )
    model_width = residual.shape[1]
    experts_total = router.shape[1]
    capacity = 2 * token_count * TOP // experts_total
    slice_width = model_width // lax.axis_size("head")
    slice_start = lax.axis_index("head") * slice_width
    projected = lax.psum(partial_out.astype(jnp.bfloat16), "head").astype(jnp.float32)
    mixed_rows = (residual.astype(jnp.float32) + projected).astype(jnp.bfloat16)
    mixed_wide = mixed_rows.astype(jnp.float32)
    inv_rms = lax.rsqrt(jnp.mean(mixed_wide * mixed_wide, axis=1, keepdims=True) + 1e-06)
    scaled = mixed_wide * moe_gain[None, :]
    moe_in = (scaled * inv_rms).astype(jnp.bfloat16)
    logits = inv_rms * jnp.dot(scaled, router, precision=PRECISE)
    base_slice = lax.dynamic_slice_in_dim(mixed_wide, slice_start, slice_width, 1)
    gate_weights, slot_index = route_tokens(logits, expert_ids, experts_total)
    target = (expert_ids * capacity + slot_index).reshape(-1)
    width_here = moe_in.shape[1]
    source = jnp.repeat(moe_in, TOP, axis=0)
    packed = jnp.zeros((experts_total * capacity, width_here), jnp.bfloat16).at[target].set(source)
    arrived = lax.all_to_all(
        packed.reshape(experts_total, capacity, width_here),
        "ctx",
        split_axis=0,
        concat_axis=0,
        tiled=True,
    )
    flat_rows = arrived.reshape(-1, model_width)
    gate_part = jnp.dot(flat_rows, w_gate[0], preferred_element_type=jnp.float32)
    up_part = jnp.dot(flat_rows, w_up[0], preferred_element_type=jnp.float32)
    hidden = (jax.nn.silu(gate_part) * up_part).astype(jnp.bfloat16)
    partial_down = jnp.dot(hidden, w_down[0], preferred_element_type=jnp.float32).reshape(
        arrived.shape
    )
    returned = lax.all_to_all(
        lax.all_to_all(
            partial_down.astype(jnp.bfloat16)[None], "ctx", split_axis=1, concat_axis=1, tiled=True
        ),
        "head",
        split_axis=3,
        concat_axis=0,
        tiled=True,
    )
    expert_out = jnp.sum(returned.astype(jnp.float32), axis=0).astype(jnp.bfloat16)
    lookup = expert_out.reshape(experts_total * capacity, slice_width)
    picked = lookup[target].reshape(token_count, TOP, slice_width).astype(jnp.float32)
    final_out = (
        base_slice + gate_weights[:, 0:1] * picked[:, 0] + gate_weights[:, 1:2] * picked[:, 1]
    )
    return final_out.astype(jnp.bfloat16)


MESH = pl.DeviceIdType.MESH
ANY = pl.BlockSpec(memory_space=pl.ANY)
VMEM = pl.BlockSpec(memory_space=pltpu.VMEM)


def plane_peers():
    me = lax.axis_index("ctx")
    core, x, y = me % 2, (me // 2) % 2, me // 4

    def at(c, a, b):
        return (b * 2 + a) * 2 + c

    return (
        me,
        at(1 - core, x, y),
        at(core, 1 - x, y),
        at(core, x, 1 - y),
        at(core, 1 - x, 1 - y),
    )


def greet(axes_and_peers):
    barrier = pltpu.get_barrier_semaphore()
    for axis, peer in axes_and_peers:
        pl.semaphore_signal(barrier, inc=1, device_id={axis: peer}, device_id_type=MESH)
    pl.semaphore_wait(barrier, len(axes_and_peers))


def block_order(me, sib, xn, yn, dg):
    def other_core(index):
        return index + 1 - 2 * (index % 2)

    return (me, sib, xn, yn, other_core(xn), other_core(yn), dg, other_core(dg))


def z_order():
    z = lax.axis_index("head")
    return (z + 1 - 2 * (z % 2), z + 2 - 4 * (z // 2), 3 - z)


def sender(send, recv):
    def copy(at, src, dst, axis, peer):
        return pltpu.make_async_remote_copy(
            src_ref=src,
            dst_ref=dst,
            send_sem=send.at[at],
            recv_sem=recv.at[at],
            device_id={axis: peer},
            device_id_type=MESH,
        )

    return copy


STATES, GATHER, TO_Z, TO_COLS = 0, 9, 18, 66
ROWS_Z, BASE_Z, SPREAD, PAIR, SUMS, SLICES, COPIES = 82, 88, 91, 163, 167, 191, 194
TILE = 256


def gather_plan(copy, first, buffer, split, peers):
    me, sib, xn, yn, dg = peers
    top, low = pl.ds(0, split), pl.ds(split, buffer.shape[1] - split)
    return [
        copy(first, buffer.at[me], buffer.at[me], "ctx", sib),
        copy(first + 1, buffer.at[me], buffer.at[me], "ctx", xn),
        copy(first + 2, buffer.at[me], buffer.at[me], "ctx", yn),
        copy(first + 3, buffer.at[xn, top], buffer.at[xn, top], "ctx", yn),
        copy(first + 4, buffer.at[xn], buffer.at[xn], "ctx", sib),
        copy(first + 5, buffer.at[yn, low], buffer.at[yn, low], "ctx", xn),
        copy(first + 6, buffer.at[yn], buffer.at[yn], "ctx", sib),
        copy(first + 7, buffer.at[dg, top], buffer.at[dg, top], "ctx", sib),
        copy(first + 8, buffer.at[dg, low], buffer.at[dg, low], "ctx", sib),
    ]


def attend(query, key, value, log_decay, attn_gain, states, rows, copy, peers):
    f32, bf16 = jnp.float32, jnp.bfloat16
    me = peers[0]
    heads, length = log_decay.shape
    size = query.shape[1] // heads
    row = lax.broadcasted_iota(jnp.int32, (length, length), 0)
    col = lax.broadcasted_iota(jnp.int32, (length, length), 1)
    causal = col <= row
    lower = causal.astype(f32)
    decay = log_decay[...]
    across = (((1,), (1,)), ((), ()))
    by_row = lax.dot_general(
        decay, lower, across, precision=PRECISE, preferred_element_type=f32
    )
    by_col = lax.dot_general(
        lower, decay, across, precision=PRECISE, preferred_element_type=f32
    )
    final = by_row[:, length - 1 :]
    for h in range(heads):
        cols = slice(h * size, (h + 1) * size)
        tail = jnp.exp(by_col[length - 1 :, h : h + 1] - by_col[:, h : h + 1])
        state = lax.dot_general(
            (key[:, cols].astype(f32) * tail).astype(bf16),
            value[:, cols],
            (((0,), (0,)), ((), ())),
            preferred_element_type=f32,
        )
        states[me, h * size : (h + 1) * size] = state.astype(bf16)
    big = final.astype(bf16).astype(f32)
    middle = (final - big).astype(bf16).astype(f32)
    small = final - big - middle
    lane = lax.broadcasted_iota(jnp.int32, (heads, size), 1)
    notes = jnp.zeros((heads, size), f32)
    for k, term in enumerate((big, middle, small)):
        notes = jnp.where(lane == k, term, notes)
    notes = jnp.concatenate([notes, jnp.zeros((16 - heads, size), f32)], axis=0)
    states[me, heads * size :] = notes.astype(bf16)

    plan = gather_plan(copy, STATES, states, heads * size // 2, peers)
    for step in (1, 2, 0):
        plan[step].start()
    inside = []
    for h in range(heads):
        cols = slice(h * size, (h + 1) * size)
        scores = lax.dot_general(
            query[:, cols], key[:, cols], across, preferred_element_type=f32
        )
        spread = jnp.where(causal, by_col[:, h : h + 1] - by_row[h : h + 1], 0.0)
        scores *= jnp.where(causal, jnp.exp(spread), 0.0)
        inside.append(
            jnp.dot(scores.astype(bf16), value[:, cols], preferred_element_type=f32)
        )
    for got, onward in ((1, (3, 4)), (2, (5, 6)), (3, (7,)), (5, (8,))):
        plan[got].wait_recv()
        for step in onward:
            plan[step].start()
    for step in (0, 4, 6, 7, 8):
        plan[step].wait_recv()

    scales = [None] * states.shape[0]
    after = jnp.zeros((heads, 1), f32)
    for k in reversed(range(states.shape[0])):
        said = states[k, heads * size :].astype(f32)[:heads]
        scales[k] = jnp.where(k < me, jnp.exp(after), 0.0)
        after += jnp.where(k < me, said[:, 0:1] + said[:, 1:2] + said[:, 2:3], 0.0)
    for h in range(heads):
        cols = slice(h * size, (h + 1) * size)
        prior = jnp.zeros((size, size), f32)
        for k in range(states.shape[0]):
            prior += scales[k][h : h + 1] * states[k, h * size : (h + 1) * size].astype(f32)
        outside = jnp.dot(query[:, cols], prior.astype(bf16), preferred_element_type=f32)
        attended = inside[h] + jnp.exp(by_col[:, h : h + 1]) * outside
        square_mean = jnp.mean(attended * attended, axis=1, keepdims=True)
        normed = attended * lax.rsqrt(square_mean + 1e-05) * attn_gain[:, cols]
        rows[me, :, cols] = normed.astype(bf16)
    return plan


def layer_kernel(
    query, key, value, log_decay, attn_gain, weight, residual, gain, router, ids,
    w_gate, w_up, w_down, out,
    states, rows, part, from_z, summed, by_cols, mixed, base, toks,
    wide, down, picked, slot_gate, hidden, theirs, ours, pair, onehots,
    ahead, across, landed, total, slices, send, recv, load,
):
    peers = plane_peers()
    me, sib, xn, yn, dg = peers
    z = lax.axis_index("head")
    blocks, zs = block_order(*peers), z_order()
    chunks = zs + (z,)
    units = hidden.shape[1]
    tiles = units // TILE
    weight_loads = []
    for j in range(tiles):
        for k, matrix in enumerate((w_gate, w_up)):
            weight_loads.append(
                pltpu.make_async_copy(
                    matrix.at[:, pl.ds(j * TILE, TILE)],
                    wide.at[2 * j + k],
                    load.at[2 * j + k],
                )
            )
    rest = units - tiles * TILE
    for k, matrix in enumerate((w_gate, w_up)):
        weight_loads.append(
            pltpu.make_async_copy(
                matrix.at[:, pl.ds(tiles * TILE, rest)],
                wide.at[2 * tiles, :, pl.ds(k * rest, rest)],
                load.at[2 * tiles + k],
            )
        )
    down_load = pltpu.make_async_copy(w_down, down, load.at[2 + 2 * tiles])
    for each in weight_loads + [down_load]:
        each.start()
    greet([("ctx", b) for b in blocks[1:]] + [("head", p) for p in zs])
    copy = sender(send, recv)
    f32, bf16 = jnp.float32, jnp.bfloat16
    model_width = residual.shape[1]
    share = residual.shape[0] // (len(zs) + 1)
    part_rows = share // 2

    def rows_at(plane, t):
        start = pl.multiple_of(plane * share + t * part_rows, part_rows)
        return pl.ds(start, part_rows)

    width = weight.shape[1]

    sent = attend(
        query, key, value, log_decay, attn_gain, states, rows, copy, peers
    )
    plan = gather_plan(copy, GATHER, rows, rows.shape[1] // 2, peers)
    for step in (1, 2, 0):
        plan[step].start()
    sent = sent + plan
    z_in = ([], [])

    def send_z(i, t):
        rows_t = pl.ds(t * part_rows, part_rows)
        z_in[t].append([])
        for d, peer in enumerate(zs):
            out_copy = copy(
                TO_Z + 6 * i + 3 * t + d,
                part.at[i, peer, rows_t],
                from_z.at[i, d, rows_t],
                "head",
                peer,
            )
            out_copy.start()
            z_in[t][i].append(out_copy)
            sent.append(out_copy)

    def project(i, block):
        product = jnp.dot(block, weight[...], preferred_element_type=f32).astype(bf16)
        for k in range(len(zs) + 1):
            part[i, k] = product[k * share : (k + 1) * share]
        send_z(i, 0)

    def arrived(*steps):
        for step in steps:
            plan[step].wait_recv()

    project(0, rows[me])
    arrived(0)
    project(1, rows[sib])
    arrived(1)
    plan[3].start()
    plan[4].start()
    project(2, rows[xn])
    arrived(2)
    plan[5].start()
    plan[6].start()
    project(3, rows[yn])
    arrived(4)
    project(4, rows[blocks[4]])
    arrived(6)
    project(5, rows[blocks[5]])
    arrived(3)
    plan[7].start()
    arrived(5)
    plan[8].start()
    project(6, rows[dg])
    arrived(7, 8)
    project(7, rows[blocks[7]])

    for i in range(len(blocks)):
        send_z(i, 1)
    col_copies = ([], [])

    def to_columns(t):
        rows_t = pl.ds(t * part_rows, part_rows)
        for i, block in enumerate(blocks):
            block_sum = part[i, z, rows_t].astype(f32)
            for d in range(3):
                z_in[t][i][d].wait_recv()
                block_sum += from_z[i, d, rows_t].astype(f32)
            summed[i, rows_t] = block_sum.astype(bf16)
            if i:
                col_copies[t].append(
                    copy(
                        TO_COLS + 8 * t + i,
                        summed.at[i, rows_t],
                        by_cols.at[me, rows_t],
                        "ctx",
                        block,
                    )
                )
                col_copies[t][-1].start()
        by_cols[me, rows_t] = summed[0, rows_t]

    def normalize(t):
        rows_t, mine = pl.ds(t * part_rows, part_rows), rows_at(z, t)
        for each in col_copies[t]:
            each.wait_recv()
        per = model_width // (len(zs) + 1) // width
        squares = jnp.zeros((part_rows, 1), f32)
        for k in range(model_width // width):
            cols = slice(k * width, (k + 1) * width)
            whole = residual[mine, cols].astype(f32) + by_cols[k, rows_t].astype(f32)
            whole = whole.astype(bf16)
            mixed[k // per, rows_t, (k % per) * width : (k % per + 1) * width] = whole
            row_values = whole.astype(f32)
            squares += jnp.sum(row_values * row_values, axis=1, keepdims=True)
        inv_rms = lax.rsqrt(squares / model_width + 1e-06)
        experts_total = router.shape[0]
        logits = [jnp.zeros((part_rows, 1), f32)] * experts_total
        slice_width = per * width
        for k in range(len(zs) + 1):
            cols = slice(k * slice_width, (k + 1) * slice_width)
            scaled = mixed[k, rows_t].astype(f32) * gain[:, cols]
            toks[me, mine, cols] = (scaled * inv_rms).astype(bf16)
            for e in range(experts_total):
                logits[e] += jnp.sum(scaled * router[e : e + 1, cols], axis=1, keepdims=True)
        named = ids[mine]
        first, second = named[:, 0:1], named[:, 1:2]
        margin = jnp.zeros((part_rows, 1), f32)
        for e in range(experts_total):
            margin += jnp.where(first == e, logits[e], 0.0)
            margin -= jnp.where(second == e, logits[e], 0.0)
        leading = jax.nn.sigmoid(margin * inv_rms)
        big = leading.astype(bf16).astype(f32)
        middle = (leading - big).astype(bf16).astype(f32)
        small = leading - big - middle
        lane = lax.broadcasted_iota(jnp.int32, (part_rows, 128), 1)
        notes = jnp.zeros((part_rows, 128), f32)
        for k, term in enumerate((first.astype(f32), second.astype(f32), big, middle, small)):
            notes = jnp.where(lane == k, term, notes)
        toks[me, mine, model_width:] = notes.astype(bf16)
        base[mine] = mixed[z, rows_t]

    z_copies, base_copies = ([], []), []
    full = toks.shape[2]
    middle_col = full // 256 * 128
    left, right = pl.ds(0, middle_col), pl.ds(middle_col, full - middle_col)

    def spread(t, j, plane):
        s = SPREAD + 9 * (4 * t + j)
        rows_of = rows_at(plane, t)

        def send_on(step, block, peer, cols=pl.ds(0, full)):
            ref = toks.at[block, rows_of, cols]
            return copy(s + step, ref, ref, "ctx", peer)

        steps = [
            send_on(0, me, sib),
            send_on(1, me, xn),
            send_on(2, me, yn),
            send_on(3, xn, yn, left),
            send_on(4, xn, sib),
            send_on(5, yn, xn, right),
            send_on(6, yn, sib),
            send_on(7, dg, sib, left),
            send_on(8, dg, sib, right),
        ]
        for step in (1, 2, 0):
            steps[step].start()
        return steps

    def begin_rows(t):
        ref = toks.at[me, rows_at(z, t)]
        for d, peer in enumerate(zs):
            z_copies[t].append(copy(ROWS_Z + 3 * t + d, ref, ref, "head", peer))
            z_copies[t][-1].start()
        return spread(t, 0, z)

    def relay(steps):
        for got, onward in ((1, (3, 4)), (2, (5, 6)), (3, (7,)), (5, (8,))):
            steps[got].wait_recv()
            for step in onward:
                steps[step].start()

    to_columns(0)
    normalize(0)
    runs = [begin_rows(0)]
    relay(runs[0])
    to_columns(1)
    normalize(1)
    runs.append(begin_rows(1))
    for t in range(2):
        for d, peer in enumerate(zs):
            z_copies[t][d].wait_recv()
            runs.append(spread(t, d + 1, peer))
            relay(runs[-2])
    own_rows = pl.ds(pl.multiple_of(z * share, share), share)
    for d, peer in enumerate(zs):
        base_copies.append(copy(BASE_Z + d, mixed.at[peer], base.at[own_rows], "head", peer))
        base_copies[-1].start()
    relay(runs[-1])
    for steps in runs:
        for step in (0, 4, 6, 7, 8):
            steps[step].wait_recv()
        sent += steps
    for each in base_copies:
        each.wait_recv()
    sent += col_copies[0] + col_copies[1] + z_copies[0] + z_copies[1] + base_copies

    count = picked.shape[0] // 4
    row = lax.broadcasted_iota(jnp.int32, (128, 128), 0)
    col = lax.broadcasted_iota(jnp.int32, (128, 128), 1)
    lower = (col <= row).astype(bf16)

    def chosen(notes, expert, offset):
        e = expert.astype(f32)
        named = (notes[:, 0:1] == e) | (notes[:, 1:2] == e)
        marks = jnp.broadcast_to(named.astype(f32), (128, 128)).astype(bf16)
        slot = jnp.dot(lower, marks, preferred_element_type=f32).astype(jnp.int32) - 1 + offset
        return jnp.where((slot == col) & (marks > 0), 1.0, 0.0)

    width = out.shape[1]
    away = (blocks[7], blocks[4], blocks[5], sib)
    here = (dg, xn, yn, me)
    pairs = [copy(PAIR + i, theirs.at[i], pair.at[i], "ctx", sib) for i in range(4)]

    def act(gated, up):
        return (gated * jax.nn.sigmoid(gated) * up).astype(bf16)

    def experts(group):
        both = (2 * group, 2 * group + 1)
        for n, block in enumerate([away[i] for i in both] + [here[i] for i in both]):
            notes = toks[block, :, model_width:].astype(f32)
            place = chosen(notes, me, 0)
            if n >= 2:
                onehots[both[n - 2]] = (place + chosen(notes, sib, count)).astype(bf16)
            pick = place[:, :count].astype(bf16)
            found = lax.dot_general(
                pick, toks[block], (((0,), (0,)), ((), ())), preferred_element_type=f32
            )
            picked[n * count : (n + 1) * count] = found[:, :model_width].astype(bf16)
            said = found[:, model_width:]
            leading = said[:, 2:3] + said[:, 3:4] + said[:, 4:5]
            gate = jnp.where(said[:, 0:1] == me.astype(f32), leading, 1.0 - leading)
            slot_gate[n * count : (n + 1) * count] = jnp.broadcast_to(gate, (count, 128))
        for j in range(tiles):
            if group == 0:
                weight_loads[2 * j].wait()
                weight_loads[2 * j + 1].wait()
            gated = jnp.dot(picked[...], wide[2 * j], preferred_element_type=f32)
            up = jnp.dot(picked[...], wide[2 * j + 1], preferred_element_type=f32)
            hidden[:, j * TILE : (j + 1) * TILE] = act(gated, up)
        if group == 0:
            weight_loads[2 * tiles].wait()
            weight_loads[2 * tiles + 1].wait()
            down_load.wait()
        last = jnp.dot(picked[...], wide[2 * tiles], preferred_element_type=f32)
        hidden[:, tiles * TILE :] = act(last[:, :rest], last[:, rest:])
        for k in range(4):
            cols = slice(k * width, (k + 1) * width)
            result = jnp.dot(hidden[...], down[:, cols], preferred_element_type=f32)
            result = (result * slot_gate[:, 0:1]).astype(bf16)
            for n in range(2):
                theirs[both[n], k] = result[n * count : (n + 1) * count]
                ours[both[n], k] = result[(n + 2) * count : (n + 3) * count]
        for i in both:
            pairs[i].start()

    half = 64
    top, low = pl.ds(0, half), pl.ds(half, half)

    def tokens_of(i, k, rows):
        slots = jnp.concatenate([ours[i, k], pair[i, k]], axis=0)
        return jnp.dot(onehots[i, rows], slots, preferred_element_type=f32)

    plans = []
    for j in range(4):
        s = SUMS + 6 * j
        plans.append(
            [
                copy(s, ahead.at[j, 0, top], across.at[j, 0], "ctx", yn),
                copy(s + 1, ahead.at[j, 0, low], across.at[j, 1], "ctx", xn),
                copy(s + 2, ahead.at[j, 1, low], landed.at[j, 0, low], "ctx", xn),
                copy(s + 3, ahead.at[j, 2, top], landed.at[j, 1, top], "ctx", yn),
                copy(s + 4, ahead.at[j, 1, top], landed.at[j, 0, top], "ctx", xn),
                copy(s + 5, ahead.at[j, 2, low], landed.at[j, 1, low], "ctx", yn),
            ]
        )
    out_z = [
        copy(SLICES + d, total.at[d], slices.at[d], "head", peer) for d, peer in enumerate(zs)
    ]

    def begin(j):
        k = chunks[j]
        ahead[j, 0] = tokens_of(0, k, slice(None)).astype(bf16)
        plans[j][0].start()
        plans[j][1].start()
        ahead[j, 1, low] = tokens_of(1, k, low).astype(bf16)
        plans[j][2].start()

    def begin_y(j):
        ahead[j, 2, top] = tokens_of(2, chunks[j], top).astype(bf16)
        plans[j][3].start()

    def pass_on(j):
        k = chunks[j]
        plans[j][0].wait_recv()
        ahead[j, 1, top] = (tokens_of(1, k, top) + across[j, 0].astype(f32)).astype(bf16)
        plans[j][4].start()
        plans[j][1].wait_recv()
        ahead[j, 2, low] = (tokens_of(2, k, low) + across[j, 1].astype(f32)).astype(bf16)
        plans[j][5].start()

    def finish(j):
        k = chunks[j]
        value = tokens_of(3, k, slice(None))
        for step in (2, 3, 4, 5):
            plans[j][step].wait_recv()
        value += landed[j, 0].astype(f32) + landed[j, 1].astype(f32)
        if j < 3:
            total[j] = value.astype(bf16)
            out_z[j].start()
        return value

    experts(0)
    pairs[0].wait_recv()
    pairs[1].wait_recv()
    for j in range(4):
        begin(j)
    experts(1)
    pairs[2].wait_recv()
    begin_y(0)
    begin_y(1)
    pass_on(0)
    begin_y(2)
    pass_on(1)
    pairs[3].wait_recv()
    finish(0)
    begin_y(3)
    pass_on(2)
    finish(1)
    pass_on(3)
    finish(2)
    value = finish(3) + base[...].astype(f32)
    for d in range(3):
        out_z[d].wait_recv()
        value += slices[d].astype(f32)
    out[...] = value.astype(bf16)
    for each in sent + pairs + sum(plans, []) + out_z:
        each.wait_send()


def layer(tensors, weights, capacity):
    ctx, planes = lax.axis_size("ctx"), lax.axis_size("head")
    query, decay, weight, residual = tensors[0], tensors[3], tensors[5], tensors[6]
    tokens, depth = query.shape
    width = weight.shape[1]
    model_width = residual.shape[1]
    share = tokens // planes
    units = weights[0].shape[1]
    part_width = model_width // planes
    tiles = units // TILE
    dma, bf16 = pltpu.SemaphoreType.DMA, jnp.bfloat16
    return pl.pallas_call(
        layer_kernel,
        out_shape=jax.ShapeDtypeStruct((tokens, part_width), bf16),
        in_specs=[VMEM] * len(tensors) + [ANY] * len(weights),
        out_specs=VMEM,
        scratch_shapes=[
            pltpu.VMEM((ctx, depth + 16, depth // decay.shape[0]), bf16),
            pltpu.VMEM((ctx, tokens, depth), bf16),
            pltpu.VMEM((ctx, planes, share, width), bf16),
            pltpu.VMEM((ctx, planes - 1, share, width), bf16),
            pltpu.VMEM((ctx, share, width), bf16),
            pltpu.VMEM((ctx, share, width), bf16),
            pltpu.VMEM((planes, share, part_width), bf16),
            pltpu.VMEM((tokens, part_width), bf16),
            pltpu.VMEM((ctx, tokens, model_width + 128), bf16),
            pltpu.VMEM((2 * tiles + 1, model_width, TILE), bf16),
            pltpu.VMEM((units, model_width), bf16),
            pltpu.VMEM((ctx // 2 * capacity, model_width), bf16),
            pltpu.VMEM((ctx // 2 * capacity, 128), jnp.float32),
            pltpu.VMEM((ctx // 2 * capacity, units), bf16),
            pltpu.VMEM((4, planes, capacity, part_width), bf16),
            pltpu.VMEM((4, planes, capacity, part_width), bf16),
            pltpu.VMEM((4, planes, capacity, part_width), bf16),
            pltpu.VMEM((4, tokens, 2 * capacity), bf16),
            pltpu.VMEM((planes, 3, tokens, part_width), bf16),
            pltpu.VMEM((planes, 2, tokens // 2, part_width), bf16),
            pltpu.VMEM((planes, 2, tokens, part_width), bf16),
            pltpu.VMEM((planes - 1, tokens, part_width), bf16),
            pltpu.VMEM((planes - 1, tokens, part_width), bf16),
            dma((COPIES,)),
            dma((COPIES,)),
            dma((3 + 2 * tiles,)),
        ],
        compiler_params=pltpu.CompilerParams(
            collective_id=1, has_side_effects=True, vmem_limit_bytes=62 << 20
        ),
        name="layer",
    )(*tensors, *weights)


def plane_body(
    query_vectors,
    key_vectors,
    value_vectors,
    log_decay,
    residual,
    out_weight,
    attn_gain,
    moe_gain,
    router,
    w_gate,
    w_up,
    w_down,
    expert_ids,
):
    token_count = query_vectors.shape[0]
    tensors = (
        query_vectors,
        key_vectors,
        value_vectors,
        log_decay,
        attn_gain[None, :],
        out_weight,
        residual,
        moe_gain[None, :],
        router.T,
        expert_ids,
    )
    capacity = 2 * token_count * TOP // router.shape[1]
    return layer(tensors, (w_gate[0], w_up[0], w_down[0]), capacity)


def solution(mesh):
    sizes = dict(mesh.shape)
    body = plane_body if (sizes["ctx"], sizes["head"]) == (8, 4) else general_body
    in_specs = (
        P("ctx", "head"),
        P("ctx", "head"),
        P("ctx", "head"),
        P("head", "ctx"),
        P("ctx", None),
        P("head", "ctx"),
        P("head"),
        P(),
        P(),
        P("ctx", None, "head"),
        P("ctx", None, "head"),
        P("ctx", "head", None),
        P("ctx", None),
    )
    out_specs = P("ctx", "head")
    return jax.shard_map(body, mesh=mesh, in_specs=in_specs, out_specs=out_specs, check_vma=False)
```

```python
import functools

import jax
import jax.numpy as jnp
from jax import lax
from jax.experimental import pallas as pl
from jax.experimental.pallas import tpu as pltpu
from jax.sharding import PartitionSpec as P

TOP = 2


PRECISE = lax.Precision.HIGHEST


def entering(value, axis, combine, identity):
    peers, index = (lax.axis_size(axis), lax.axis_index(axis))
    everything = jax.tree.map(
        lambda part, kind: lax.all_gather(part.astype(kind), axis),
        value,
        (jnp.bfloat16, jnp.bfloat16),
    )
    start = jax.tree.map(
        lambda part, zero: jnp.broadcast_to(jnp.asarray(zero, part.dtype), part.shape),
        value,
        identity,
    )

    def step(k, before):
        reached = k < index
        new = combine(
            before, jax.tree.map(lambda part, own: part[k].astype(own.dtype), everything, value)
        )
        return jax.tree.map(lambda a, b: jnp.where(reached, a, b), new, before)

    return lax.fori_loop(0, peers, step, start)


def local_attention(query_block, key_block, value_block, decay_block):
    running = jnp.cumsum(decay_block, axis=1)
    length_here = decay_block.shape[1]
    row_index = lax.broadcasted_iota(jnp.int32, (length_here, length_here), 0)
    col_index = lax.broadcasted_iota(jnp.int32, (length_here, length_here), 1)
    causal = (col_index <= row_index)[None]
    spread = jnp.where(causal, running[:, :, None] - running[:, None, :], 0.0)
    decay_weights = jnp.where(causal, jnp.exp(spread), 0.0)
    scores = jnp.einsum("htd,hsd->hts", query_block, key_block, precision=PRECISE) * decay_weights
    inside_part = jnp.einsum("hts,hse->hte", scores, value_block, precision=PRECISE)
    final_log = running[:, -1]
    tail_decay = jnp.exp(final_log[:, None] - running)
    local_state = jnp.einsum(
        "hsd,hse->hde", key_block * tail_decay[:, :, None], value_block, precision=PRECISE
    )
    return (inside_part, running, local_state, final_log)


def route_tokens(logits, expert_ids, experts_total):
    onehot = expert_ids[:, :, None] == lax.broadcasted_iota(jnp.int32, (1, 1, experts_total), 2)
    chosen = jnp.sum(jnp.where(onehot, logits[:, None, :], 0.0), axis=2)
    leading = jax.nn.sigmoid(chosen[:, 0] - chosen[:, 1])
    gate_weights = jnp.stack([leading, 1.0 - leading], axis=1)
    marked = onehot.reshape(-1, experts_total).astype(jnp.int32)
    earlier = jnp.cumsum(marked, axis=0) - marked
    slot_index = jnp.sum(earlier * marked, axis=1).reshape(expert_ids.shape)
    return (gate_weights, slot_index)


def link_states(earlier, later):
    return (earlier[0] + later[0], jnp.exp(later[0])[:, None, None] * earlier[1] + later[1])


def general_body(
    query_vectors,
    key_vectors,
    value_vectors,
    log_decay,
    residual,
    out_weight,
    attn_gain,
    moe_gain,
    router,
    w_gate,
    w_up,
    w_down,
    expert_ids,
):
    token_count = query_vectors.shape[0]
    heads_here = log_decay.shape[0]
    head_size = query_vectors.shape[1] // heads_here

    def split_heads(matrix_in):
        return (
            matrix_in.astype(jnp.float32)
            .reshape(token_count, heads_here, head_size)
            .transpose(1, 0, 2)
        )

    query_heads = split_heads(query_vectors)
    inside_part, running, local_state, final_log = local_attention(
        query_heads, split_heads(key_vectors), split_heads(value_vectors), log_decay
    )
    identity = (jnp.zeros_like(final_log), jnp.zeros_like(local_state))
    _, prior_state = entering((final_log, local_state), "ctx", link_states, identity)
    outside_part = jnp.exp(running)[:, :, None] * jnp.einsum(
        "htd,hde->hte", query_heads, prior_state, precision=PRECISE
    )
    attended = inside_part + outside_part
    square_mean = jnp.mean(attended * attended, axis=2, keepdims=True)
    heads_normed = (
        attended * lax.rsqrt(square_mean + 1e-05) * attn_gain.reshape(heads_here, 1, head_size)
    )
    heads_normed = (
        heads_normed.astype(jnp.bfloat16)
        .transpose(1, 0, 2)
        .reshape(token_count, heads_here * head_size)
    )
    partial_out = jnp.dot(
        heads_normed,
        lax.all_gather(out_weight, "ctx", axis=1, tiled=True),
        preferred_element_type=jnp.float32,
    )
    model_width = residual.shape[1]
    experts_total = router.shape[1]
    capacity = 2 * token_count * TOP // experts_total
    slice_width = model_width // lax.axis_size("head")
    slice_start = lax.axis_index("head") * slice_width
    projected = lax.psum(partial_out.astype(jnp.bfloat16), "head").astype(jnp.float32)
    mixed_rows = (residual.astype(jnp.float32) + projected).astype(jnp.bfloat16)
    mixed_wide = mixed_rows.astype(jnp.float32)
    inv_rms = lax.rsqrt(jnp.mean(mixed_wide * mixed_wide, axis=1, keepdims=True) + 1e-06)
    scaled = mixed_wide * moe_gain[None, :]
    moe_in = (scaled * inv_rms).astype(jnp.bfloat16)
    logits = inv_rms * jnp.dot(scaled, router, precision=PRECISE)
    base_slice = lax.dynamic_slice_in_dim(mixed_wide, slice_start, slice_width, 1)
    gate_weights, slot_index = route_tokens(logits, expert_ids, experts_total)
    target = (expert_ids * capacity + slot_index).reshape(-1)
    width_here = moe_in.shape[1]
    source = jnp.repeat(moe_in, TOP, axis=0)
    packed = jnp.zeros((experts_total * capacity, width_here), jnp.bfloat16).at[target].set(source)
    arrived = lax.all_to_all(
        packed.reshape(experts_total, capacity, width_here),
        "ctx",
        split_axis=0,
        concat_axis=0,
        tiled=True,
    )
    flat_rows = arrived.reshape(-1, model_width)
    gate_part = jnp.dot(flat_rows, w_gate[0], preferred_element_type=jnp.float32)
    up_part = jnp.dot(flat_rows, w_up[0], preferred_element_type=jnp.float32)
    hidden = (jax.nn.silu(gate_part) * up_part).astype(jnp.bfloat16)
    partial_down = jnp.dot(hidden, w_down[0], preferred_element_type=jnp.float32).reshape(
        arrived.shape
    )
    returned = lax.all_to_all(
        lax.all_to_all(
            partial_down.astype(jnp.bfloat16)[None], "ctx", split_axis=1, concat_axis=1, tiled=True
        ),
        "head",
        split_axis=3,
        concat_axis=0,
        tiled=True,
    )
    expert_out = jnp.sum(returned.astype(jnp.float32), axis=0).astype(jnp.bfloat16)
    lookup = expert_out.reshape(experts_total * capacity, slice_width)
    picked = lookup[target].reshape(token_count, TOP, slice_width).astype(jnp.float32)
    final_out = (
        base_slice + gate_weights[:, 0:1] * picked[:, 0] + gate_weights[:, 1:2] * picked[:, 1]
    )
    return final_out.astype(jnp.bfloat16)


MESH = pl.DeviceIdType.MESH
ANY = pl.BlockSpec(memory_space=pl.ANY)
VMEM = pl.BlockSpec(memory_space=pltpu.VMEM)


def plane_peers():
    me = lax.axis_index("ctx")
    core, x, y = me % 2, (me // 2) % 2, me // 4

    def at(c, a, b):
        return (b * 2 + a) * 2 + c

    return (
        me,
        at(1 - core, x, y),
        at(core, 1 - x, y),
        at(core, x, 1 - y),
        at(core, 1 - x, 1 - y),
    )


def greet(axes_and_peers):
    barrier = pltpu.get_barrier_semaphore()
    for axis, peer in axes_and_peers:
        pl.semaphore_signal(barrier, inc=1, device_id={axis: peer}, device_id_type=MESH)
    pl.semaphore_wait(barrier, len(axes_and_peers))


def block_order(me, sib, xn, yn, dg):
    def other_core(index):
        return index + 1 - 2 * (index % 2)

    return (me, sib, xn, yn, other_core(xn), other_core(yn), dg, other_core(dg))


def z_order():
    z = lax.axis_index("head")
    return (z + 1 - 2 * (z % 2), z + 2 - 4 * (z // 2), 3 - z)


def sender(send, recv):
    def copy(at, src, dst, axis, peer):
        return pltpu.make_async_remote_copy(
            src_ref=src,
            dst_ref=dst,
            send_sem=send.at[at],
            recv_sem=recv.at[at],
            device_id={axis: peer},
            device_id_type=MESH,
        )

    return copy


STATES, GATHER, TO_Z, TO_COLS = 0, 9, 18, 42
ROWS_Z, BASE_Z, SPREAD, PAIR, SUMS, SLICES, COPIES = 50, 53, 56, 92, 96, 120, 123
TILE = 256


def gather_plan(copy, first, buffer, split, peers):
    me, sib, xn, yn, dg = peers
    top, low = pl.ds(0, split), pl.ds(split, buffer.shape[1] - split)
    return [
        copy(first, buffer.at[me], buffer.at[me], "ctx", sib),
        copy(first + 1, buffer.at[me], buffer.at[me], "ctx", xn),
        copy(first + 2, buffer.at[me], buffer.at[me], "ctx", yn),
        copy(first + 3, buffer.at[xn, top], buffer.at[xn, top], "ctx", yn),
        copy(first + 4, buffer.at[xn], buffer.at[xn], "ctx", sib),
        copy(first + 5, buffer.at[yn, low], buffer.at[yn, low], "ctx", xn),
        copy(first + 6, buffer.at[yn], buffer.at[yn], "ctx", sib),
        copy(first + 7, buffer.at[dg], buffer.at[dg], "ctx", sib),
    ]


def attend(query, key, value, log_decay, attn_gain, states, rows, copy, peers):
    f32, bf16 = jnp.float32, jnp.bfloat16
    me = peers[0]
    heads, length = log_decay.shape
    size = query.shape[1] // heads
    row = lax.broadcasted_iota(jnp.int32, (length, length), 0)
    col = lax.broadcasted_iota(jnp.int32, (length, length), 1)
    causal = col <= row
    lower = causal.astype(f32)
    decay = log_decay[...]
    across = (((1,), (1,)), ((), ()))
    by_row = lax.dot_general(
        decay, lower, across, precision=PRECISE, preferred_element_type=f32
    )
    by_col = lax.dot_general(
        lower, decay, across, precision=PRECISE, preferred_element_type=f32
    )
    final = by_row[:, length - 1 :]
    for h in range(heads):
        cols = slice(h * size, (h + 1) * size)
        tail = jnp.exp(by_col[length - 1 :, h : h + 1] - by_col[:, h : h + 1])
        state = lax.dot_general(
            (key[:, cols].astype(f32) * tail).astype(bf16),
            value[:, cols],
            (((0,), (0,)), ((), ())),
            preferred_element_type=f32,
        )
        states[me, h * size : (h + 1) * size] = state.astype(bf16)
    big = final.astype(bf16).astype(f32)
    middle = (final - big).astype(bf16).astype(f32)
    small = final - big - middle
    lane = lax.broadcasted_iota(jnp.int32, (heads, size), 1)
    notes = jnp.zeros((heads, size), f32)
    for k, term in enumerate((big, middle, small)):
        notes = jnp.where(lane == k, term, notes)
    notes = jnp.concatenate([notes, jnp.zeros((16 - heads, size), f32)], axis=0)
    states[me, heads * size :] = notes.astype(bf16)

    plan = gather_plan(copy, STATES, states, heads * size // 2, peers)
    for step in (1, 2, 0):
        plan[step].start()
    inside = []
    for h in range(heads):
        cols = slice(h * size, (h + 1) * size)
        scores = lax.dot_general(
            query[:, cols], key[:, cols], across, preferred_element_type=f32
        )
        spread = jnp.where(causal, by_col[:, h : h + 1] - by_row[h : h + 1], 0.0)
        scores *= jnp.where(causal, jnp.exp(spread), 0.0)
        inside.append(
            jnp.dot(scores.astype(bf16), value[:, cols], preferred_element_type=f32)
        )
    for got, onward in ((1, (3, 4)), (2, (5, 6)), (3, ()), (5, (7,))):
        plan[got].wait_recv()
        for step in onward:
            plan[step].start()
    for step in (0, 4, 6, 7):
        plan[step].wait_recv()

    scales = [None] * states.shape[0]
    after = jnp.zeros((heads, 1), f32)
    for k in reversed(range(states.shape[0])):
        said = states[k, heads * size :].astype(f32)[:heads]
        scales[k] = jnp.where(k < me, jnp.exp(after), 0.0)
        after += jnp.where(k < me, said[:, 0:1] + said[:, 1:2] + said[:, 2:3], 0.0)
    for h in range(heads):
        cols = slice(h * size, (h + 1) * size)
        prior = jnp.zeros((size, size), f32)
        for k in range(states.shape[0]):
            prior += scales[k][h : h + 1] * states[k, h * size : (h + 1) * size].astype(f32)
        outside = jnp.dot(query[:, cols], prior.astype(bf16), preferred_element_type=f32)
        attended = inside[h] + jnp.exp(by_col[:, h : h + 1]) * outside
        square_mean = jnp.mean(attended * attended, axis=1, keepdims=True)
        normed = attended * lax.rsqrt(square_mean + 1e-05) * attn_gain[:, cols]
        rows[me, :, cols] = normed.astype(bf16)
    return plan


def layer_kernel(
    query, key, value, log_decay, attn_gain, weight, residual, gain, router, ids,
    w_gate, w_up, w_down, out,
    states, rows, part, from_z, summed, by_cols, mixed, base, toks,
    wide, down, picked, slot_gate, hidden, theirs, ours, pair, onehots,
    ahead, across, landed, total, slices, send, recv, load,
):
    peers = plane_peers()
    me, sib, xn, yn, dg = peers
    z = lax.axis_index("head")
    blocks, zs = block_order(*peers), z_order()
    chunks = zs + (z,)
    units = hidden.shape[1]
    tiles = units // TILE
    weight_loads = []
    for j in range(tiles):
        for k, matrix in enumerate((w_gate, w_up)):
            weight_loads.append(
                pltpu.make_async_copy(
                    matrix.at[:, pl.ds(j * TILE, TILE)],
                    wide.at[2 * j + k],
                    load.at[2 * j + k],
                )
            )
    rest = units - tiles * TILE
    for k, matrix in enumerate((w_gate, w_up)):
        weight_loads.append(
            pltpu.make_async_copy(
                matrix.at[:, pl.ds(tiles * TILE, rest)],
                wide.at[2 * tiles, :, pl.ds(k * rest, rest)],
                load.at[2 * tiles + k],
            )
        )
    down_load = pltpu.make_async_copy(w_down, down, load.at[2 + 2 * tiles])
    for each in weight_loads + [down_load]:
        each.start()
    greet([("ctx", b) for b in blocks[1:]] + [("head", p) for p in zs])
    copy = sender(send, recv)
    f32, bf16 = jnp.float32, jnp.bfloat16
    model_width = residual.shape[1]
    share = residual.shape[0] // (len(zs) + 1)
    mine = pl.ds(pl.multiple_of(z * share, share), share)
    width = weight.shape[1]

    sent = attend(
        query, key, value, log_decay, attn_gain, states, rows, copy, peers
    )
    plan = gather_plan(copy, GATHER, rows, rows.shape[1] // 2, peers)
    for step in (1, 2, 0):
        plan[step].start()
    sent = sent + plan
    z_in = []

    def project(i, block):
        product = jnp.dot(block, weight[...], preferred_element_type=f32).astype(bf16)
        for k in range(len(zs) + 1):
            part[k, i] = product[k * share : (k + 1) * share]
        if i % 2 == 0:
            return
        two = pl.ds(i - 1, 2)
        z_in.append([])
        for d, peer in enumerate(zs):
            out_copy = copy(
                TO_Z + 3 * (i // 2) + d, part.at[peer, two], from_z.at[d, two], "head", peer
            )
            out_copy.start()
            z_in[-1].append(out_copy)
            sent.append(out_copy)

    def arrived(*steps):
        for step in steps:
            plan[step].wait_recv()

    project(0, rows[me])
    arrived(0)
    project(1, rows[sib])
    arrived(1)
    plan[3].start()
    plan[4].start()
    project(2, rows[xn])
    arrived(2)
    plan[5].start()
    plan[6].start()
    project(3, rows[yn])
    arrived(4)
    project(4, rows[blocks[4]])
    arrived(6)
    project(5, rows[blocks[5]])
    arrived(3, 5)
    plan[7].start()
    project(6, rows[dg])
    arrived(7)
    project(7, rows[blocks[7]])

    col_copies = []
    for i, block in enumerate(blocks):
        block_sum = part[z, i].astype(f32)
        for d in range(3):
            if i % 2 == 0:
                z_in[i // 2][d].wait_recv()
            block_sum += from_z[d, i].astype(f32)
        summed[i] = block_sum.astype(bf16)
        if i:
            col_copies.append(
                copy(TO_COLS + i, summed.at[i], by_cols.at[me], "ctx", block)
            )
            col_copies[-1].start()
    by_cols[me] = summed[0]
    for each in col_copies:
        each.wait_recv()
    sent += col_copies

    per = model_width // (len(zs) + 1) // width
    squares = jnp.zeros((share, 1), f32)
    for k in range(model_width // width):
        cols = slice(k * width, (k + 1) * width)
        whole = (residual[mine, cols].astype(f32) + by_cols[k].astype(f32)).astype(bf16)
        mixed[k // per, :, (k % per) * width : (k % per + 1) * width] = whole
        row_values = whole.astype(f32)
        squares += jnp.sum(row_values * row_values, axis=1, keepdims=True)
    inv_rms = lax.rsqrt(squares / model_width + 1e-06)
    experts_total = router.shape[0]
    logits = [jnp.zeros((share, 1), f32)] * experts_total
    slice_width = per * width
    for k in range(len(zs) + 1):
        cols = slice(k * slice_width, (k + 1) * slice_width)
        scaled = mixed[k].astype(f32) * gain[:, cols]
        toks[me, mine, cols] = (scaled * inv_rms).astype(bf16)
        for e in range(experts_total):
            logits[e] += jnp.sum(scaled * router[e : e + 1, cols], axis=1, keepdims=True)
    first, second = ids[:, 0:1], ids[:, 1:2]
    margin = jnp.zeros((share, 1), f32)
    for e in range(experts_total):
        margin += jnp.where(first == e, logits[e], 0.0) - jnp.where(second == e, logits[e], 0.0)
    leading = jax.nn.sigmoid(margin * inv_rms)
    big = leading.astype(bf16).astype(f32)
    middle = (leading - big).astype(bf16).astype(f32)
    small = leading - big - middle
    lane = lax.broadcasted_iota(jnp.int32, (share, 128), 1)
    notes = jnp.zeros((share, 128), f32)
    for k, value in enumerate((first.astype(f32), second.astype(f32), big, middle, small)):
        notes = jnp.where(lane == k, value, notes)
    toks[me, mine, model_width:] = notes.astype(bf16)
    base[mine] = mixed[z]

    z_copies, base_copies = [], []
    quarter = share // 2

    def spread(j, k):
        s = SPREAD + 9 * j
        start = pl.multiple_of(k * share, share)
        rows_of = pl.ds(start, share)
        upper, lower = pl.ds(start, quarter), pl.ds(start + quarter, quarter)

        def send_on(step, block, part_of, peer):
            ref = toks.at[block, part_of]
            return copy(s + step, ref, ref, "ctx", peer)

        steps = [
            send_on(0, me, rows_of, sib),
            send_on(1, me, rows_of, xn),
            send_on(2, me, rows_of, yn),
            send_on(3, xn, upper, yn),
            send_on(4, xn, rows_of, sib),
            send_on(5, yn, lower, xn),
            send_on(6, yn, rows_of, sib),
            send_on(7, dg, rows_of, sib),
        ]
        for step in (1, 2, 0):
            steps[step].start()
        return steps

    def relay(steps):
        for got, onward in ((1, (3, 4)), (2, (5, 6)), (3, ()), (5, (7,))):
            steps[got].wait_recv()
            for step in onward:
                steps[step].start()

    for d, peer in enumerate(zs):
        z_copies.append(
            copy(ROWS_Z + d, toks.at[me, mine], toks.at[me, mine], "head", peer)
        )
        z_copies[-1].start()
    runs = [spread(0, z)]
    for d, peer in enumerate(zs):
        z_copies[d].wait_recv()
        runs.append(spread(d + 1, peer))
        relay(runs[d])
    for d, peer in enumerate(zs):
        base_copies.append(copy(BASE_Z + d, mixed.at[peer], base.at[mine], "head", peer))
        base_copies[-1].start()
    relay(runs[3])
    for steps in runs:
        for step in (0, 4, 6, 7):
            steps[step].wait_recv()
        sent += steps
    for each in base_copies:
        each.wait_recv()
    sent += z_copies + base_copies

    count = picked.shape[0] // 4
    row = lax.broadcasted_iota(jnp.int32, (128, 128), 0)
    col = lax.broadcasted_iota(jnp.int32, (128, 128), 1)
    lower = (col <= row).astype(bf16)

    def chosen(notes, expert, offset):
        e = expert.astype(f32)
        named = (notes[:, 0:1] == e) | (notes[:, 1:2] == e)
        marks = jnp.broadcast_to(named.astype(f32), (128, 128)).astype(bf16)
        slot = jnp.dot(lower, marks, preferred_element_type=f32).astype(jnp.int32) - 1 + offset
        return jnp.where((slot == col) & (marks > 0), 1.0, 0.0)

    width = out.shape[1]
    away = (blocks[7], blocks[4], blocks[5], sib)
    here = (dg, xn, yn, me)
    pairs = [copy(PAIR + i, theirs.at[i], pair.at[i], "ctx", sib) for i in range(4)]

    def act(gated, up):
        return (gated * jax.nn.sigmoid(gated) * up).astype(bf16)

    def experts(group):
        both = (2 * group, 2 * group + 1)
        for n, block in enumerate([away[i] for i in both] + [here[i] for i in both]):
            notes = toks[block, :, model_width:].astype(f32)
            place = chosen(notes, me, 0)
            if n >= 2:
                onehots[both[n - 2]] = (place + chosen(notes, sib, count)).astype(bf16)
            pick = place[:, :count].astype(bf16)
            found = lax.dot_general(
                pick, toks[block], (((0,), (0,)), ((), ())), preferred_element_type=f32
            )
            picked[n * count : (n + 1) * count] = found[:, :model_width].astype(bf16)
            said = found[:, model_width:]
            leading = said[:, 2:3] + said[:, 3:4] + said[:, 4:5]
            gate = jnp.where(said[:, 0:1] == me.astype(f32), leading, 1.0 - leading)
            slot_gate[n * count : (n + 1) * count] = jnp.broadcast_to(gate, (count, 128))
        for j in range(tiles):
            if group == 0:
                weight_loads[2 * j].wait()
                weight_loads[2 * j + 1].wait()
            gated = jnp.dot(picked[...], wide[2 * j], preferred_element_type=f32)
            up = jnp.dot(picked[...], wide[2 * j + 1], preferred_element_type=f32)
            hidden[:, j * TILE : (j + 1) * TILE] = act(gated, up)
        if group == 0:
            weight_loads[2 * tiles].wait()
            weight_loads[2 * tiles + 1].wait()
            down_load.wait()
        last = jnp.dot(picked[...], wide[2 * tiles], preferred_element_type=f32)
        hidden[:, tiles * TILE :] = act(last[:, :rest], last[:, rest:])
        for k in range(4):
            cols = slice(k * width, (k + 1) * width)
            result = jnp.dot(hidden[...], down[:, cols], preferred_element_type=f32)
            result = (result * slot_gate[:, 0:1]).astype(bf16)
            for n in range(2):
                theirs[both[n], k] = result[n * count : (n + 1) * count]
                ours[both[n], k] = result[(n + 2) * count : (n + 3) * count]
        for i in both:
            pairs[i].start()

    half = 64
    top, low = pl.ds(0, half), pl.ds(half, half)

    def tokens_of(i, k, rows):
        slots = jnp.concatenate([ours[i, k], pair[i, k]], axis=0)
        return jnp.dot(onehots[i, rows], slots, preferred_element_type=f32)

    plans = []
    for j in range(4):
        s = SUMS + 6 * j
        plans.append(
            [
                copy(s, ahead.at[j, 0, top], across.at[j, 0], "ctx", yn),
                copy(s + 1, ahead.at[j, 0, low], across.at[j, 1], "ctx", xn),
                copy(s + 2, ahead.at[j, 1, low], landed.at[j, 0, low], "ctx", xn),
                copy(s + 3, ahead.at[j, 2, top], landed.at[j, 1, top], "ctx", yn),
                copy(s + 4, ahead.at[j, 1, top], landed.at[j, 0, top], "ctx", xn),
                copy(s + 5, ahead.at[j, 2, low], landed.at[j, 1, low], "ctx", yn),
            ]
        )
    out_z = [
        copy(SLICES + d, total.at[d], slices.at[d], "head", peer) for d, peer in enumerate(zs)
    ]

    def begin(j):
        k = chunks[j]
        ahead[j, 0] = tokens_of(0, k, slice(None)).astype(bf16)
        plans[j][0].start()
        plans[j][1].start()
        ahead[j, 1, low] = tokens_of(1, k, low).astype(bf16)
        plans[j][2].start()

    def begin_y(j):
        ahead[j, 2, top] = tokens_of(2, chunks[j], top).astype(bf16)
        plans[j][3].start()

    def pass_on(j):
        k = chunks[j]
        plans[j][0].wait_recv()
        ahead[j, 1, top] = (tokens_of(1, k, top) + across[j, 0].astype(f32)).astype(bf16)
        plans[j][4].start()
        plans[j][1].wait_recv()
        ahead[j, 2, low] = (tokens_of(2, k, low) + across[j, 1].astype(f32)).astype(bf16)
        plans[j][5].start()

    def finish(j):
        k = chunks[j]
        value = tokens_of(3, k, slice(None))
        for step in (2, 3, 4, 5):
            plans[j][step].wait_recv()
        value += landed[j, 0].astype(f32) + landed[j, 1].astype(f32)
        if j < 3:
            total[j] = value.astype(bf16)
            out_z[j].start()
        return value

    experts(0)
    pairs[0].wait_recv()
    pairs[1].wait_recv()
    for j in range(4):
        begin(j)
    experts(1)
    pairs[2].wait_recv()
    begin_y(0)
    begin_y(1)
    pass_on(0)
    begin_y(2)
    pass_on(1)
    pairs[3].wait_recv()
    finish(0)
    begin_y(3)
    pass_on(2)
    finish(1)
    pass_on(3)
    finish(2)
    value = finish(3) + base[...].astype(f32)
    for d in range(3):
        out_z[d].wait_recv()
        value += slices[d].astype(f32)
    out[...] = value.astype(bf16)
    for each in sent + pairs + sum(plans, []) + out_z:
        each.wait_send()


def layer(tensors, weights, capacity):
    ctx, planes = lax.axis_size("ctx"), lax.axis_size("head")
    query, decay, weight, residual = tensors[0], tensors[3], tensors[5], tensors[6]
    tokens, depth = query.shape
    width = weight.shape[1]
    model_width = residual.shape[1]
    share = tokens // planes
    units = weights[0].shape[1]
    part_width = model_width // planes
    tiles = units // TILE
    dma, bf16 = pltpu.SemaphoreType.DMA, jnp.bfloat16
    return pl.pallas_call(
        layer_kernel,
        out_shape=jax.ShapeDtypeStruct((tokens, part_width), bf16),
        in_specs=[VMEM] * len(tensors) + [ANY] * len(weights),
        out_specs=VMEM,
        scratch_shapes=[
            pltpu.VMEM((ctx, depth + 16, depth // decay.shape[0]), bf16),
            pltpu.VMEM((ctx, tokens, depth), bf16),
            pltpu.VMEM((planes, ctx, share, width), bf16),
            pltpu.VMEM((planes - 1, ctx, share, width), bf16),
            pltpu.VMEM((ctx, share, width), bf16),
            pltpu.VMEM((ctx, share, width), bf16),
            pltpu.VMEM((planes, share, part_width), bf16),
            pltpu.VMEM((tokens, part_width), bf16),
            pltpu.VMEM((ctx, tokens, model_width + 128), bf16),
            pltpu.VMEM((2 * tiles + 1, model_width, TILE), bf16),
            pltpu.VMEM((units, model_width), bf16),
            pltpu.VMEM((ctx // 2 * capacity, model_width), bf16),
            pltpu.VMEM((ctx // 2 * capacity, 128), jnp.float32),
            pltpu.VMEM((ctx // 2 * capacity, units), bf16),
            pltpu.VMEM((4, planes, capacity, part_width), bf16),
            pltpu.VMEM((4, planes, capacity, part_width), bf16),
            pltpu.VMEM((4, planes, capacity, part_width), bf16),
            pltpu.VMEM((4, tokens, 2 * capacity), bf16),
            pltpu.VMEM((planes, 3, tokens, part_width), bf16),
            pltpu.VMEM((planes, 2, tokens // 2, part_width), bf16),
            pltpu.VMEM((planes, 2, tokens, part_width), bf16),
            pltpu.VMEM((planes - 1, tokens, part_width), bf16),
            pltpu.VMEM((planes - 1, tokens, part_width), bf16),
            dma((COPIES,)),
            dma((COPIES,)),
            dma((3 + 2 * tiles,)),
        ],
        compiler_params=pltpu.CompilerParams(
            collective_id=1, has_side_effects=True, vmem_limit_bytes=62 << 20
        ),
        name="layer",
    )(*tensors, *weights)


def plane_body(
    query_vectors,
    key_vectors,
    value_vectors,
    log_decay,
    residual,
    out_weight,
    attn_gain,
    moe_gain,
    router,
    w_gate,
    w_up,
    w_down,
    expert_ids,
):
    token_count = query_vectors.shape[0]
    z, planes = lax.axis_index("head"), lax.axis_size("head")
    share = token_count // planes
    tensors = (
        query_vectors,
        key_vectors,
        value_vectors,
        log_decay,
        attn_gain[None, :],
        out_weight,
        residual,
        moe_gain[None, :],
        router.T,
        lax.dynamic_slice_in_dim(expert_ids, z * share, share, 0),
    )
    capacity = 2 * token_count * TOP // router.shape[1]
    return layer(tensors, (w_gate[0], w_up[0], w_down[0]), capacity)


def solution(mesh):
    sizes = dict(mesh.shape)
    body = plane_body if (sizes["ctx"], sizes["head"]) == (8, 4) else general_body
    in_specs = (
        P("ctx", "head"),
        P("ctx", "head"),
        P("ctx", "head"),
        P("head", "ctx"),
        P("ctx", None),
        P("head", "ctx"),
        P("head"),
        P(),
        P(),
        P("ctx", None, "head"),
        P("ctx", None, "head"),
        P("ctx", "head", None),
        P("ctx", None),
    )
    out_specs = P("ctx", "head")
    return jax.shard_map(body, mesh=mesh, in_specs=in_specs, out_specs=out_specs, check_vma=False)
```
